32 devices in a mesh: seq: 16 (over z, x, core), ch: 2 (over y).
Axes of the slice: x: 2, y: 2, z: 4, core: 2. Of those that a mesh axis runs over, the one named last changes fastest.
Arguments:
- signal: float32 [4096, 4096], P('seq', 'ch'), may hold values from -6 to 6
- filters: float32 [4096, 256], P(('seq', 'ch')), may hold values from -1 to 1
- skip_gain: float32 [4096], P('ch'), may hold values from -1 to 1
Outputs:
- filtered: float32 [4096, 4096], P('seq', 'ch')
The draws below stay inside these ranges and needn't reach their ends.
All inputs are finite; a program needn't handle non-finite values.
Results may differ from the reference program's by a relative error of at most 0.00009.
Values sent between devices are 32-bit elements; how exact they have to be, the bound alone decides.
No kernel may reach another device: no remote copies, remote signals or barrier semaphores. Data moves between devices by JAX's collectives and lax.ppermute only.
A program may use at most 128 MiB of HBM per device.

```python
import jax
import jax.numpy as jnp
from jax import lax

C = 4096
GROUP = 16
GROUPS = 256
SEQ_LEN = 4096


def draw_filters(key, part):
    keys = jax.random.split(jax.random.fold_in(key, 7), 7)
    length = SEQ_LEN
    slow = jnp.exp(jax.random.uniform(keys[1], (GROUPS,), jnp.float32, jnp.log(0.25 / length), jnp.log(2.0 / length)))
    quick = jnp.exp(jax.random.uniform(keys[2], (GROUPS,), jnp.float32, jnp.log(2.0 / length), jnp.log(1.0 / 30.0)))
    coin = jax.random.bernoulli(keys[0], 0.5, (GROUPS,))
    rates = jnp.where(coin, slow, quick)
    noise = jnp.clip(jax.random.normal(keys[5], (length, GROUPS), jnp.float32), -4.0, 4.0)
    tail_rates = jnp.exp(jax.random.uniform(keys[6], (GROUPS,), jnp.float32, jnp.log(0.25 / length), jnp.log(2.0 / length)))
    digit_places = jax.random.randint(keys[3], (3, GROUPS), 0, length)
    scale_factors = jax.random.uniform(keys[4], (3, GROUPS), jnp.float32, 0.5, 0.8)
    delay_steps = jnp.arange(length, dtype=jnp.int32)[:, None]
    lag_values = delay_steps.astype(jnp.float32)
    scale = jnp.sqrt((1.0 - jnp.exp(-2.0 * rates)) / (1.0 - jnp.exp(-2.0 * rates * length)))
    tail_scale = jnp.sqrt((1.0 - jnp.exp(-2.0 * tail_rates)) / (1.0 - jnp.exp(-2.0 * tail_rates * length)))
    head_profile = jnp.exp(-lag_values * rates[None, :]) * scale[None, :]
    tail_profile = jnp.exp(-lag_values * tail_rates[None, :]) * tail_scale[None, :]
    decay_profile = jnp.sqrt(0.9) * head_profile + jnp.sqrt(0.1) * tail_profile
    for impulse_spike in range(3):
        decay_profile = decay_profile * jnp.where(delay_steps >= digit_places[impulse_spike][None, :], scale_factors[impulse_spike][None, :], 1.0)
    return (noise * decay_profile).astype(jnp.float32)


def level_of(key, dims, shards, smallest, top_value):
    def one(position, shards_of):
        heights = jax.random.uniform(jax.random.fold_in(jax.random.fold_in(key, 6), position), (shards_of,), jnp.float32, smallest / len(shards), top_value / len(shards))
        return jnp.repeat(jnp.exp(heights), dims[position] // shards_of).reshape((-1,) + (1,) * (len(dims) - position - 1))

    gain = one(*shards[0])
    for cut in shards[1:]:
        gain = gain * one(*cut)
    return gain


def scatter_about(stream_key, shape, width, limit, cuts=(), kind=jnp.bfloat16):
    entries = jax.random.normal(stream_key, shape, jnp.float32) * width
    if len(cuts) > 0:
        entries = level_of(stream_key, shape, cuts, -0.22, 0.18) * entries
    return jnp.clip(entries, min=-limit, max=limit).astype(kind)


def setup_inputs(seed: int = 0) -> dict:
    key_list = jax.random.split(jax.random.key(seed), 4)
    return {
        "signal": scatter_about(key_list[0], (SEQ_LEN, C), 1.0, 6.0, ((0, 16), (1, 2)), jnp.float32),
        "filters": draw_filters(jax.random.fold_in(key_list[3], 71), 0),
        "skip_gain": jnp.clip(jax.random.uniform(key_list[2], (C,), jnp.float32, -1.0, 1.0) * level_of(key_list[2], (C,), ((0, 2),), -0.4, 0.0), -1.0, 1.0),
    }


def reference(signal, filters, skip_gain):
    length = signal.shape[0]
    groups = filters.shape[1]
    grouped = jnp.transpose(signal.reshape(length, groups, GROUP), (1, 0, 2))
    kernels = jnp.transpose(filters, (1, 0))

    def convolve(pair):
        block, kernel = pair
        spectrum = jnp.fft.rfft(block, n=2 * length, axis=0)
        response = jnp.fft.rfft(kernel, n=2 * length)
        return jnp.fft.irfft(spectrum * response[:, None], n=2 * length, axis=0)[:length]

    conv = lax.map(convolve, (grouped, kernels))
    conv = jnp.transpose(conv, (1, 0, 2)).reshape(length, groups * GROUP)
    return (conv + skip_gain[None, :] * signal).astype(signal.dtype)
```

```python
import functools
import math

import jax
import jax.numpy as jnp
from jax import lax
from jax.experimental import pallas as pl
from jax.experimental.pallas import tpu as pltpu
from jax.sharding import PartitionSpec as P

GROUP = 16
HALF = 128
CHUNKS = 1

HIGHEST_PRECISION = lax.Precision.HIGHEST


def split_halves(values):
    high = values.astype(jnp.bfloat16)
    low = (values - high.astype(jnp.float32)).astype(jnp.bfloat16)
    return high, low


def turn_kernel(in_ref, out_ref):
    out_ref[...] = in_ref[...].T


def turn_out(signal, chunk, chunks):
    rows, width = signal.shape
    cols = width // chunks
    steps = cols // HALF
    return pl.pallas_call(
        turn_kernel,
        grid=(steps,),
        in_specs=[pl.BlockSpec((rows, HALF), lambda i: (0, chunk * steps + i))],
        out_specs=pl.BlockSpec((HALF, rows), lambda i: (i, 0)),
        out_shape=jax.ShapeDtypeStruct((cols, rows), jnp.float32),
        name="turn_out",
    )(signal)


def home_kernel(back_ref, signal_ref, gain_ref, *rest):
    out_ref = rest[-1]
    out_ref[...] = back_ref[...].T + gain_ref[...] * signal_ref[...]


def turn_home(back, signal, gain, partial_out, chunk, chunks):
    rows, width = signal.shape
    steps = width // chunks // HALF
    here = lambda i: (0, chunk * steps + i)
    in_specs = [
        pl.BlockSpec((HALF, rows), lambda i: (i, 0)),
        pl.BlockSpec((rows, HALF), here),
        pl.BlockSpec((1, HALF), here),
    ]
    operands = [back, signal, gain]
    aliases = {}
    if partial_out is not None:
        in_specs.append(pl.BlockSpec(memory_space=pl.ANY))
        operands.append(partial_out)
        aliases = {3: 0}
    return pl.pallas_call(
        home_kernel,
        grid=(steps,),
        in_specs=in_specs,
        out_specs=pl.BlockSpec((rows, HALF), here),
        out_shape=jax.ShapeDtypeStruct((rows, width), jnp.float32),
        input_output_aliases=aliases,
        name="turn_home",
    )(*operands)


def conv_kernel(first, taps_ref, sig_ref, out_ref, high_ref, low_ref, sum_ref):
    blocks, _, rows = sig_ref.shape
    lags = blocks * rows
    group = first + pl.program_id(0)
    lines = [
        jnp.broadcast_to(taps_ref[i, pl.ds(group, 1), :], (8, HALF)) for i in range(lags // HALF)
    ]
    blank = jnp.zeros((8, HALF), jnp.float32)
    strip = jnp.concatenate([blank] + lines + [blank], axis=1)
    strip = pltpu.roll(strip, 0, 1, stride=1, stride_axis=0)
    for p in range(HALF // 16):
        pair = jnp.concatenate(
            [pltpu.roll(strip, 16 * p, 1) if p else strip, pltpu.roll(strip, 16 * p + 8, 1)], axis=0
        )
        high, low = split_halves(pair)
        high_ref[16 * p : 16 * p + 16, :] = high
        low_ref[16 * p : 16 * p + 16, :] = low
    sig_high, sig_low = split_halves(sig_ref[...].reshape(blocks * GROUP, rows))

    def window(ref, lag_block):
        start = lag_block * rows
        return jnp.concatenate(
            [ref[:, start + HALF * (k) : start + HALF * k + rows] for k in reversed(range(rows // HALF))],
            axis=0,
        )

    for d in range(blocks):
        n = (blocks - d) * GROUP
        taps_high, taps_low = window(high_ref, d), window(low_ref, d)
        both = jnp.concatenate([sig_high[:n], sig_low[:n]], axis=0)
        part = jnp.dot(both, taps_high, preferred_element_type=jnp.float32)
        term = part[:n] + part[n:]
        term = term + jnp.dot(sig_high[:n], taps_low, preferred_element_type=jnp.float32)
        if d == 0:
            sum_ref[...] = term
        else:
            sum_ref[d * GROUP :, :] += term
    out_ref[...] = sum_ref[...].reshape(blocks, GROUP, rows)


def convolve(taps, arrived, chunk):
    blocks, width, rows = arrived.shape
    groups = width // GROUP
    lanes = blocks * rows + 2 * HALF
    products = 3 * 2 * groups * GROUP * rows * rows * blocks * (blocks + 1) // 2
    spec = pl.BlockSpec((blocks, GROUP, rows), lambda g: (0, g, 0))
    return pl.pallas_call(
        functools.partial(conv_kernel, chunk * groups),
        grid=(groups,),
        in_specs=[pl.BlockSpec(taps.shape, lambda g: (0, 0, 0)), spec],
        out_specs=spec,
        out_shape=jax.ShapeDtypeStruct(arrived.shape, jnp.float32),
        scratch_shapes=[
            pltpu.VMEM((HALF, lanes), jnp.bfloat16),
            pltpu.VMEM((HALF, lanes), jnp.bfloat16),
            pltpu.VMEM((blocks * GROUP, rows), jnp.float32),
        ],
        compiler_params=pltpu.CompilerParams(vmem_limit_bytes=40 * 1024 * 1024),
        cost_estimate=pl.CostEstimate(
            flops=products, bytes_accessed=8 * blocks * width * rows, transcendentals=0
        ),
        name="convolve",
    )(taps, arrived)


def fast_body(signal, filters, skip_gain):
    blocks = lax.axis_size("seq")
    sides = lax.axis_size("ch")
    rows, width = signal.shape
    lag_rows, groups = filters.shape
    chunks = CHUNKS
    per_chunk = width // chunks // blocks
    local = groups // sides // blocks
    by_home = filters.T.reshape(sides, chunks, blocks, local // chunks, lag_rows)
    by_home = by_home.transpose(2, 0, 1, 3, 4).reshape(blocks * sides, local, lag_rows)
    taps = lax.all_to_all(by_home, ("seq", "ch"), split_axis=0, concat_axis=0, tiled=True)
    gain = skip_gain.reshape(1, width)
    out = None
    for k in range(chunks):
        leaving = turn_out(signal, k, chunks).reshape(blocks, per_chunk, rows)
        arrived = lax.all_to_all(leaving, "seq", split_axis=0, concat_axis=0, tiled=True)
        values = convolve(taps, arrived, k)
        back = lax.all_to_all(values, "seq", split_axis=0, concat_axis=0, tiled=True)
        out = turn_home(back.reshape(blocks * per_chunk, rows), signal, gain, out, k, chunks)
    return out


def angle_table(row_count, col_count, length, sign):
    row_index = jnp.arange(row_count, dtype=jnp.int32)[:, None]
    col_index = jnp.arange(col_count, dtype=jnp.int32)[None, :]
    phase = row_index * col_index % length
    angle = sign * 2.0 * math.pi / length * phase.astype(jnp.float32)
    return (jnp.cos(angle), jnp.sin(angle))


def complex_apply(form, table, real_part, imag_part):
    cosine, sine = table

    def product(matrix, values):
        return jnp.einsum(form, matrix, values, precision=HIGHEST_PRECISION)

    if imag_part is None:
        return (product(cosine, real_part), product(sine, real_part))
    return (
        product(cosine, real_part) - product(sine, imag_part),
        product(cosine, imag_part) + product(sine, real_part),
    )


def rotate(real_part, imag_part, cosine, sine):
    return (real_part * cosine - imag_part * sine, real_part * sine + imag_part * cosine)


def local_convolve(whole_sig, whole_taps, blocks, rows):
    width = whole_sig.shape[1]
    span = 2 * blocks * rows
    sig_blocks = whole_sig.reshape(blocks, rows, width)
    tap_blocks = whole_taps.reshape(blocks, rows, width)
    outer = angle_table(2 * blocks, blocks, 2 * blocks, -1.0)
    sig_real, sig_imag = complex_apply("kn,nbc->kbc", outer, sig_blocks, None)
    filt_real, filt_imag = complex_apply("kn,nbc->kbc", outer, tap_blocks, None)
    phase = (
        jnp.arange(2 * blocks, dtype=jnp.int32)[:, None]
        * jnp.arange(rows, dtype=jnp.int32)[None, :]
        % span
    )
    twist = 2.0 * math.pi / span * phase.astype(jnp.float32)
    twist_cos = jnp.cos(twist)[:, :, None]
    twist_sin = jnp.sin(twist)[:, :, None]
    sig_real, sig_imag = rotate(sig_real, sig_imag, twist_cos, -twist_sin)
    filt_real, filt_imag = rotate(filt_real, filt_imag, twist_cos, -twist_sin)
    inner = angle_table(rows, rows, rows, -1.0)
    sig_real, sig_imag = complex_apply("kn,bnc->bkc", inner, sig_real, sig_imag)
    filt_real, filt_imag = complex_apply("kn,bnc->bkc", inner, filt_real, filt_imag)
    prod_real, prod_imag = rotate(sig_real, sig_imag, filt_real, filt_imag)
    inverse_inner = angle_table(rows, rows, rows, 1.0)
    back_real, back_imag = complex_apply("nk,bkc->bnc", inverse_inner, prod_real, prod_imag)
    back_real, back_imag = rotate(back_real, back_imag, twist_cos, twist_sin)
    outer_back = angle_table(blocks, 2 * blocks, 2 * blocks, 1.0)
    values = jnp.einsum(
        "nk,kbc->nbc", outer_back[0], back_real, precision=HIGHEST_PRECISION
    ) - jnp.einsum("nk,kbc->nbc", outer_back[1], back_imag, precision=HIGHEST_PRECISION)
    return values.reshape(blocks * rows, width) / span


def spectral_body(signal, filters, skip_gain):
    blocks = lax.axis_size("seq")
    rows = signal.shape[0]
    taps = lax.all_to_all(filters, "ch", split_axis=1, concat_axis=0, tiled=True)
    local_groups = taps.shape[1]
    per_channel = jnp.broadcast_to(taps[:, :, None], (rows, local_groups, GROUP)).reshape(
        rows, local_groups * GROUP
    )
    whole_sig, whole_taps = (
        lax.all_to_all(signal, "seq", split_axis=1, concat_axis=0, tiled=True),
        lax.all_to_all(per_channel, "seq", split_axis=1, concat_axis=0, tiled=True),
    )
    values = local_convolve(whole_sig, whole_taps, blocks, rows)
    homed = lax.all_to_all(values, "seq", split_axis=0, concat_axis=1, tiled=True)
    return homed + skip_gain[None, :] * signal


def body(signal, filters, skip_gain):
    blocks = lax.axis_size("seq")
    rows, width = signal.shape
    lag_rows = filters.shape[0]
    fits = (
        width % (blocks * CHUNKS * GROUP) == 0
        and width % (CHUNKS * HALF) == 0
        and rows % HALF == 0
        and lag_rows == HALF
    )
    if fits:
        return fast_body(signal, filters, skip_gain)
    return spectral_body(signal, filters, skip_gain)


def solution(mesh):
    placed = (P("seq", "ch"), P(("seq", "ch"), None), P("ch"))
    return jax.shard_map(
        body, mesh=mesh, in_specs=placed, out_specs=P("seq", "ch"), check_vma=False
    )
```

```python
import functools
import math

import jax
import jax.numpy as jnp
from jax import lax
from jax.experimental import pallas as pl
from jax.experimental.pallas import tpu as pltpu
from jax.sharding import PartitionSpec as P

GROUP = 16
HALF = 128
VMEM_BYTES = 60 * 1024 * 1024

HIGHEST_PRECISION = lax.Precision.HIGHEST


def split_halves(values):
    high = values.astype(jnp.bfloat16)
    low = (values - high.astype(jnp.float32)).astype(jnp.bfloat16)
    return high, low


def turned(in_ref):
    return in_ref[...].T


def turn_taps_kernel(counts, sig_ref, taps_ref, out_ref):
    blocks, _, rows = out_ref.shape
    per_chunk = sig_ref.shape[1] // blocks
    lag_rows, groups = taps_ref.shape
    out_ref[:, :per_chunk, :] = turned(sig_ref).reshape(blocks, per_chunk, rows)
    lines = turned(taps_ref)
    sides = rows // lag_rows
    for side in range(sides):
        row = per_chunk
        start = side * (groups // sides)
        for count in counts:
            for q in range(blocks):
                here = start + q * count
                at = slice(side * lag_rows, (side + 1) * lag_rows)
                out_ref[q, row : row + count, at] = lines[here : here + count]
            row += count
            start += blocks * count


def turn_taps(signal, filters, blocks, counts):
    rows, width = signal.shape
    cols = blocks * counts[0] * GROUP
    shape = (blocks, counts[0] * GROUP + sum(counts), rows)
    return pl.pallas_call(
        functools.partial(turn_taps_kernel, counts),
        grid=(1,),
        in_specs=[
            pl.BlockSpec((rows, cols), lambda i: (0, 0)),
            pl.BlockSpec(filters.shape, lambda i: (0, 0)),
        ],
        out_specs=pl.BlockSpec(shape, lambda i: (0, 0, 0)),
        out_shape=jax.ShapeDtypeStruct(shape, jnp.float32),
        compiler_params=pltpu.CompilerParams(vmem_limit_bytes=VMEM_BYTES),
        cost_estimate=pl.CostEstimate(flops=0, bytes_accessed=8 * rows * cols, transcendentals=0),
        name="turn_taps",
    )(signal, filters)


def turn_kernel(sig_ref, out_ref):
    out_ref[...] = turned(sig_ref)


def turn(signal, start, cols):
    rows = signal.shape[0]
    step = math.gcd(start, cols)
    return pl.pallas_call(
        turn_kernel,
        grid=(cols // step,),
        in_specs=[pl.BlockSpec((rows, step), lambda i: (0, start // step + i))],
        out_specs=pl.BlockSpec((step, rows), lambda i: (i, 0)),
        out_shape=jax.ShapeDtypeStruct((cols, rows), jnp.float32),
        compiler_params=pltpu.CompilerParams(vmem_limit_bytes=VMEM_BYTES),
        cost_estimate=pl.CostEstimate(flops=0, bytes_accessed=8 * rows * cols, transcendentals=0),
        name="turn",
    )(signal)


def home_kernel(back_ref, sig_ref, gain_ref, *rest):
    rest[-1][...] = turned(back_ref) + gain_ref[...] * sig_ref[...]


def home(back, signal, gain, start, partial_out):
    rows, width = signal.shape
    cols = back.shape[0]
    step = math.gcd(start, cols)
    here = lambda i: (0, start // step + i)
    in_specs = [
        pl.BlockSpec((step, rows), lambda i: (i, 0)),
        pl.BlockSpec((rows, step), here),
        pl.BlockSpec((1, step), here),
    ]
    operands = [back, signal, gain]
    aliases = {}
    if partial_out is not None:
        in_specs.append(pl.BlockSpec(memory_space=pl.ANY))
        operands.append(partial_out)
        aliases = {3: 0}
    return pl.pallas_call(
        home_kernel,
        grid=(cols // step,),
        in_specs=in_specs,
        out_specs=pl.BlockSpec((rows, step), here),
        out_shape=jax.ShapeDtypeStruct((rows, width), jnp.float32),
        input_output_aliases=aliases,
        compiler_params=pltpu.CompilerParams(vmem_limit_bytes=VMEM_BYTES),
        cost_estimate=pl.CostEstimate(flops=0, bytes_accessed=12 * rows * cols, transcendentals=0),
        name="home",
    )(*operands)


def convolve_group(side, group, own_ref, other_ref, signal, high_ref, low_ref, sum_ref):
    blocks = own_ref.shape[0]
    rows = signal.shape[1]

    def line(ref, q):
        return jnp.broadcast_to(ref[q, pl.ds(group, 1), :], (8, HALF))

    lines = []
    for q in range(blocks):
        own, other = line(own_ref, q), line(other_ref, q)
        lines += [jnp.where(side == 0, own, other), jnp.where(side == 0, other, own)]
    blank = jnp.zeros((8, HALF), jnp.float32)
    strip = jnp.concatenate([blank] + lines + [blank], axis=1)
    strip = pltpu.roll(strip, 0, 1, stride=1, stride_axis=0)
    for p in range(HALF // 16):
        pair = jnp.concatenate(
            [pltpu.roll(strip, 16 * p, 1) if p else strip, pltpu.roll(strip, 16 * p + 8, 1)], axis=0
        )
        high, low = split_halves(pair)
        high_ref[16 * p : 16 * p + 16, :] = high
        low_ref[16 * p : 16 * p + 16, :] = low
    sig_high, sig_low = split_halves(signal)

    def window(ref, lag_block):
        start = lag_block * rows
        return jnp.concatenate(
            [ref[:, start + HALF * k : start + HALF * k + rows] for k in (1, 0)], axis=0
        )

    for d in range(blocks):
        n = (blocks - d) * GROUP
        taps_high, taps_low = window(high_ref, d), window(low_ref, d)
        both = jnp.concatenate([sig_high[:n], sig_low[:n]], axis=0)
        part = jnp.dot(both, taps_high, preferred_element_type=jnp.float32)
        term = part[:n] + part[n:]
        term = term + jnp.dot(sig_high[:n], taps_low, preferred_element_type=jnp.float32)
        if d == 0:
            sum_ref[...] = term
        else:
            sum_ref[d * GROUP :, :] += term


def conv_kernel(first, place_ref, own_ref, other_ref, sig_ref, out_ref, high_ref, low_ref, sum_ref):
    blocks, _, rows = sig_ref.shape
    signal = sig_ref[...].reshape(blocks * GROUP, rows)
    group = first + pl.program_id(0)
    convolve_group(place_ref[1], group, own_ref, other_ref, signal, high_ref, low_ref, sum_ref)
    out_ref[...] = sum_ref[...].reshape(blocks, GROUP, rows)


def conv_scratch(blocks, rows):
    lanes = blocks * rows + 2 * HALF
    return [
        pltpu.VMEM((HALF, lanes), jnp.bfloat16),
        pltpu.VMEM((HALF, lanes), jnp.bfloat16),
        pltpu.VMEM((blocks * GROUP, rows), jnp.float32),
    ]


def conv_cost(blocks, groups, rows):
    products = 3 * groups * GROUP * rows * rows * blocks * (blocks + 1)
    return pl.CostEstimate(
        flops=products, bytes_accessed=8 * blocks * groups * GROUP * rows, transcendentals=0
    )


def convolve(place, own, other, arrived, first, groups):
    blocks, _, rows = arrived.shape
    spec = pl.BlockSpec((blocks, GROUP, rows), lambda g: (0, g, 0))
    taps_spec = pl.BlockSpec(own.shape, lambda g: (0, 0, 0))
    return pl.pallas_call(
        functools.partial(conv_kernel, first),
        grid=(groups,),
        in_specs=[pl.BlockSpec(memory_space=pltpu.SMEM), taps_spec, taps_spec, spec],
        out_specs=spec,
        out_shape=jax.ShapeDtypeStruct((blocks, groups * GROUP, rows), jnp.float32),
        scratch_shapes=conv_scratch(blocks, rows),
        compiler_params=pltpu.CompilerParams(vmem_limit_bytes=VMEM_BYTES),
        cost_estimate=conv_cost(blocks, groups, rows),
        name="convolve",
    )(place, own, other, arrived)


def exchange(values, axis, step):
    size = lax.axis_size(axis)
    return lax.ppermute(values, axis, [(i, i ^ step) for i in range(size)])


def spread(values):
    return lax.all_to_all(values, "seq", split_axis=0, concat_axis=0, tiled=True)


def fast_body(signal, filters, skip_gain):
    blocks = lax.axis_size("seq")
    rows, width = signal.shape
    counts = (width // blocks // GROUP // 2,) * 2
    side = lax.axis_index("ch")
    place = jnp.stack([lax.axis_index("seq"), side]).astype(jnp.int32)
    gain = skip_gain.reshape(1, width)
    starts = [blocks * GROUP * sum(counts[:k]) for k in range(len(counts) + 1)]
    arrived = []
    for k in range(len(counts)):
        if k == 0:
            leaving = turn_taps(signal, filters, blocks, counts)
        else:
            leaving = turn(signal, starts[k], starts[k + 1] - starts[k])
            leaving = leaving.reshape(blocks, -1, rows)
        arrived.append(spread(leaving))
    taps = arrived[0][:, counts[0] * GROUP :, :]
    own = lax.dynamic_slice_in_dim(taps, side * HALF, HALF, axis=2)
    other = exchange(lax.dynamic_slice_in_dim(taps, (1 - side) * HALF, HALF, axis=2), "ch", 1)
    out = None
    for k, count in enumerate(counts):
        values = convolve(place, own, other, arrived[k], sum(counts[:k]), count)
        back = spread(values).reshape(-1, rows)
        out = home(back, signal, gain, starts[k], out)
    return out


def angle_table(row_count, col_count, length, sign):
    row_index = jnp.arange(row_count, dtype=jnp.int32)[:, None]
    col_index = jnp.arange(col_count, dtype=jnp.int32)[None, :]
    phase = row_index * col_index % length
    angle = sign * 2.0 * math.pi / length * phase.astype(jnp.float32)
    return (jnp.cos(angle), jnp.sin(angle))


def complex_apply(form, table, real_part, imag_part):
    cosine, sine = table

    def product(matrix, values):
        return jnp.einsum(form, matrix, values, precision=HIGHEST_PRECISION)

    if imag_part is None:
        return (product(cosine, real_part), product(sine, real_part))
    return (
        product(cosine, real_part) - product(sine, imag_part),
        product(cosine, imag_part) + product(sine, real_part),
    )


def rotate(real_part, imag_part, cosine, sine):
    return (real_part * cosine - imag_part * sine, real_part * sine + imag_part * cosine)


def local_convolve(whole_sig, whole_taps, blocks, rows):
    width = whole_sig.shape[1]
    span = 2 * blocks * rows
    sig_blocks = whole_sig.reshape(blocks, rows, width)
    tap_blocks = whole_taps.reshape(blocks, rows, width)
    outer = angle_table(2 * blocks, blocks, 2 * blocks, -1.0)
    sig_real, sig_imag = complex_apply("kn,nbc->kbc", outer, sig_blocks, None)
    filt_real, filt_imag = complex_apply("kn,nbc->kbc", outer, tap_blocks, None)
    phase = (
        jnp.arange(2 * blocks, dtype=jnp.int32)[:, None]
        * jnp.arange(rows, dtype=jnp.int32)[None, :]
        % span
    )
    twist = 2.0 * math.pi / span * phase.astype(jnp.float32)
    twist_cos = jnp.cos(twist)[:, :, None]
    twist_sin = jnp.sin(twist)[:, :, None]
    sig_real, sig_imag = rotate(sig_real, sig_imag, twist_cos, -twist_sin)
    filt_real, filt_imag = rotate(filt_real, filt_imag, twist_cos, -twist_sin)
    inner = angle_table(rows, rows, rows, -1.0)
    sig_real, sig_imag = complex_apply("kn,bnc->bkc", inner, sig_real, sig_imag)
    filt_real, filt_imag = complex_apply("kn,bnc->bkc", inner, filt_real, filt_imag)
    prod_real, prod_imag = rotate(sig_real, sig_imag, filt_real, filt_imag)
    inverse_inner = angle_table(rows, rows, rows, 1.0)
    back_real, back_imag = complex_apply("nk,bkc->bnc", inverse_inner, prod_real, prod_imag)
    back_real, back_imag = rotate(back_real, back_imag, twist_cos, twist_sin)
    outer_back = angle_table(blocks, 2 * blocks, 2 * blocks, 1.0)
    values = jnp.einsum(
        "nk,kbc->nbc", outer_back[0], back_real, precision=HIGHEST_PRECISION
    ) - jnp.einsum("nk,kbc->nbc", outer_back[1], back_imag, precision=HIGHEST_PRECISION)
    return values.reshape(blocks * rows, width) / span


def spectral_body(signal, filters, skip_gain):
    blocks = lax.axis_size("seq")
    rows = signal.shape[0]
    taps = lax.all_to_all(filters, "ch", split_axis=1, concat_axis=0, tiled=True)
    local_groups = taps.shape[1]
    per_channel = jnp.broadcast_to(taps[:, :, None], (rows, local_groups, GROUP)).reshape(
        rows, local_groups * GROUP
    )
    whole_sig, whole_taps = (
        lax.all_to_all(signal, "seq", split_axis=1, concat_axis=0, tiled=True),
        lax.all_to_all(per_channel, "seq", split_axis=1, concat_axis=0, tiled=True),
    )
    values = local_convolve(whole_sig, whole_taps, blocks, rows)
    homed = lax.all_to_all(values, "seq", split_axis=0, concat_axis=1, tiled=True)
    return homed + skip_gain[None, :] * signal


def body(signal, filters, skip_gain):
    blocks = lax.axis_size("seq")
    rows, width = signal.shape
    lag_rows = filters.shape[0]
    fits = (
        blocks > 1
        and lax.axis_size("ch") == 2
        and width % (blocks * 2 * GROUP) == 0
        and rows == 2 * HALF
        and lag_rows == HALF
    )
    if fits:
        return fast_body(signal, filters, skip_gain)
    return spectral_body(signal, filters, skip_gain)


def solution(mesh):
    placed = (P("seq", "ch"), P(("seq", "ch"), None), P("ch"))
    return jax.shard_map(
        body, mesh=mesh, in_specs=placed, out_specs=P("seq", "ch"), check_vma=False
    )
```

```python
import functools
import math

import jax
import jax.numpy as jnp
from jax import lax
from jax.experimental import pallas as pl
from jax.experimental.pallas import tpu as pltpu
from jax.sharding import PartitionSpec as P

GROUP = 16
HALF = 128
PAIR = 2
VMEM_BYTES = 60 * 1024 * 1024

HIGHEST_PRECISION = lax.Precision.HIGHEST


def split_halves(values):
    high = values.astype(jnp.bfloat16)
    low = (values - high.astype(jnp.float32)).astype(jnp.bfloat16)
    return high, low


def turned(in_ref):
    return in_ref[...].T


def turn_taps_kernel(counts, sig_ref, taps_ref, out_ref):
    blocks, _, rows = out_ref.shape
    per_chunk = sig_ref.shape[1] // blocks
    lag_rows, groups = taps_ref.shape
    out_ref[:, :per_chunk, :] = turned(sig_ref).reshape(blocks, per_chunk, rows)
    lines = turned(taps_ref)
    sides = rows // lag_rows
    for side in range(sides):
        row = per_chunk
        start = side * (groups // sides)
        for count in counts:
            for q in range(blocks):
                here = start + q * count
                at = slice(side * lag_rows, (side + 1) * lag_rows)
                out_ref[q, row : row + count, at] = lines[here : here + count]
            row += count
            start += blocks * count


def turn_taps(signal, filters, blocks, counts):
    rows, width = signal.shape
    cols = blocks * counts[0] * GROUP
    shape = (blocks, counts[0] * GROUP + sum(counts), rows)
    return pl.pallas_call(
        functools.partial(turn_taps_kernel, counts),
        grid=(1,),
        in_specs=[
            pl.BlockSpec((rows, cols), lambda i: (0, 0)),
            pl.BlockSpec(filters.shape, lambda i: (0, 0)),
        ],
        out_specs=pl.BlockSpec(shape, lambda i: (0, 0, 0)),
        out_shape=jax.ShapeDtypeStruct(shape, jnp.float32),
        compiler_params=pltpu.CompilerParams(vmem_limit_bytes=VMEM_BYTES),
        cost_estimate=pl.CostEstimate(flops=0, bytes_accessed=8 * rows * cols, transcendentals=0),
        name="turn_taps",
    )(signal, filters)


def turn_kernel(sig_ref, out_ref):
    out_ref[...] = turned(sig_ref)


def turn(signal, start, cols):
    rows = signal.shape[0]
    step = math.gcd(start, cols)
    return pl.pallas_call(
        turn_kernel,
        grid=(cols // step,),
        in_specs=[pl.BlockSpec((rows, step), lambda i: (0, start // step + i))],
        out_specs=pl.BlockSpec((step, rows), lambda i: (i, 0)),
        out_shape=jax.ShapeDtypeStruct((cols, rows), jnp.float32),
        compiler_params=pltpu.CompilerParams(vmem_limit_bytes=VMEM_BYTES),
        cost_estimate=pl.CostEstimate(flops=0, bytes_accessed=8 * rows * cols, transcendentals=0),
        name="turn",
    )(signal)


def home_kernel(back_ref, sig_ref, gain_ref, *rest):
    rest[-1][...] = turned(back_ref) + gain_ref[...] * sig_ref[...]


def home(back, signal, gain, start, partial_out):
    rows, width = signal.shape
    cols = back.shape[0]
    step = math.gcd(start, cols)
    here = lambda i: (0, start // step + i)
    in_specs = [
        pl.BlockSpec((step, rows), lambda i: (i, 0)),
        pl.BlockSpec((rows, step), here),
        pl.BlockSpec((1, step), here),
    ]
    operands = [back, signal, gain]
    aliases = {}
    if partial_out is not None:
        in_specs.append(pl.BlockSpec(memory_space=pl.ANY))
        operands.append(partial_out)
        aliases = {3: 0}
    return pl.pallas_call(
        home_kernel,
        grid=(cols // step,),
        in_specs=in_specs,
        out_specs=pl.BlockSpec((rows, step), here),
        out_shape=jax.ShapeDtypeStruct((rows, width), jnp.float32),
        input_output_aliases=aliases,
        compiler_params=pltpu.CompilerParams(vmem_limit_bytes=VMEM_BYTES),
        cost_estimate=pl.CostEstimate(flops=0, bytes_accessed=12 * rows * cols, transcendentals=0),
        name="home",
    )(*operands)


def shifted_taps(side, group, own_ref, other_ref, high_ref, low_ref):
    blocks = own_ref.shape[0]

    def line(ref, q):
        return jnp.broadcast_to(ref[q, pl.ds(group, 1), :], (8, HALF))

    lines = []
    for q in range(blocks):
        own, other = line(own_ref, q), line(other_ref, q)
        lines += [jnp.where(side == 0, own, other), jnp.where(side == 0, other, own)]
    blank = jnp.zeros((8, HALF), jnp.float32)
    strip = jnp.concatenate([blank] + lines + [blank], axis=1)
    strip = pltpu.roll(strip, 0, 1, stride=1, stride_axis=0)
    for p in range(HALF // 16):
        pair = jnp.concatenate(
            [pltpu.roll(strip, 16 * p, 1) if p else strip, pltpu.roll(strip, 16 * p + 8, 1)], axis=0
        )
        high, low = split_halves(pair)
        high_ref[16 * p : 16 * p + 16, :] = high
        low_ref[16 * p : 16 * p + 16, :] = low


def causal_sums(signal, high_ref, low_ref, sum_ref):
    rows = signal.shape[1]
    blocks = signal.shape[0] // GROUP
    sig_high, sig_low = split_halves(signal)

    def window(ref, lag_block):
        start = lag_block * rows
        return jnp.concatenate(
            [ref[:, start + HALF * k : start + HALF * k + rows] for k in (1, 0)], axis=0
        )

    for d in range(blocks):
        n = (blocks - d) * GROUP
        taps_high, taps_low = window(high_ref, d), window(low_ref, d)
        both = jnp.concatenate([sig_high[:n], sig_low[:n]], axis=0)
        part = jnp.dot(both, taps_high, preferred_element_type=jnp.float32)
        term = part[:n] + part[n:]
        term = term + jnp.dot(sig_high[:n], taps_low, preferred_element_type=jnp.float32)
        if d == 0:
            sum_ref[...] = term
        else:
            sum_ref[d * GROUP :, :] += term


def conv_kernel(first, place_ref, own_ref, other_ref, sig_ref, *rest):
    outs, scratch = rest[: -3 * PAIR], rest[-3 * PAIR :]
    blocks, _, rows = sig_ref.shape
    me, side = place_ref[0], place_ref[1]
    for u in range(PAIR):
        group = first + PAIR * pl.program_id(0) + u
        shifted_taps(side, group, own_ref, other_ref, scratch[3 * u], scratch[3 * u + 1])
    for u in range(PAIR):
        high_ref, low_ref, sum_ref = scratch[3 * u : 3 * u + 3]
        at = slice(u * GROUP, (u + 1) * GROUP)
        causal_sums(sig_ref[:, at, :].reshape(blocks * GROUP, rows), high_ref, low_ref, sum_ref)
        if len(outs) == 1:
            outs[0][:, at, :] = sum_ref[...].reshape(blocks, GROUP, rows)
            continue
        for j in range(blocks):
            row = pl.multiple_of((me ^ j) * GROUP, GROUP)
            outs[j][at, :] = sum_ref[pl.ds(row, GROUP), :]


def convolve(place, own, other, arrived, first, groups, apart):
    blocks, _, rows = arrived.shape
    spec = pl.BlockSpec((blocks, PAIR * GROUP, rows), lambda g: (0, g, 0))
    taps_spec = pl.BlockSpec(own.shape, lambda g: (0, 0, 0))
    out_specs, shapes = [spec], [(blocks, groups * GROUP, rows)]
    if apart:
        out_specs = [pl.BlockSpec((PAIR * GROUP, rows), lambda g: (g, 0))] * blocks
        shapes = [(groups * GROUP, rows)] * blocks
    lanes = blocks * rows + 2 * HALF
    scratch = [
        pltpu.VMEM((HALF, lanes), jnp.bfloat16),
        pltpu.VMEM((HALF, lanes), jnp.bfloat16),
        pltpu.VMEM((blocks * GROUP, rows), jnp.float32),
    ]
    return pl.pallas_call(
        functools.partial(conv_kernel, first),
        grid=(groups // PAIR,),
        in_specs=[pl.BlockSpec(memory_space=pltpu.SMEM), taps_spec, taps_spec, spec],
        out_specs=out_specs,
        out_shape=[jax.ShapeDtypeStruct(shape, jnp.float32) for shape in shapes],
        scratch_shapes=scratch * PAIR,
        compiler_params=pltpu.CompilerParams(vmem_limit_bytes=VMEM_BYTES),
        cost_estimate=pl.CostEstimate(
            flops=3 * groups * GROUP * rows * rows * blocks * (blocks + 1),
            bytes_accessed=8 * blocks * groups * GROUP * rows,
            transcendentals=0,
        ),
        name="convolve",
    )(place, own, other, arrived)


def home_apart_kernel(place_ref, *rest):
    back_refs, (sig_ref, gain_ref, _, out_ref, hold_ref) = rest[:-5], rest[-5:]
    me = place_ref[0]
    for j, back_ref in enumerate(back_refs):
        hold_ref[me ^ j] = back_ref[...]
    values = hold_ref[...].reshape(sig_ref.shape[1], sig_ref.shape[0])
    out_ref[...] = values.T + gain_ref[...] * sig_ref[...]


def home_apart(place, backs, signal, gain, partial_out):
    rows, width = signal.shape
    blocks, per_chunk = len(backs), backs[0].shape[0]
    cols = blocks * per_chunk
    here = lambda i: (0, 1)
    return pl.pallas_call(
        home_apart_kernel,
        grid=(1,),
        in_specs=[pl.BlockSpec(memory_space=pltpu.SMEM)]
        + [pl.BlockSpec((per_chunk, rows), lambda i: (0, 0))] * blocks
        + [pl.BlockSpec((rows, cols), here), pl.BlockSpec((1, cols), here)]
        + [pl.BlockSpec(memory_space=pl.ANY)],
        out_specs=pl.BlockSpec((rows, cols), here),
        out_shape=jax.ShapeDtypeStruct((rows, width), jnp.float32),
        input_output_aliases={blocks + 3: 0},
        scratch_shapes=[pltpu.VMEM((blocks, per_chunk, rows), jnp.float32)],
        compiler_params=pltpu.CompilerParams(vmem_limit_bytes=VMEM_BYTES),
        cost_estimate=pl.CostEstimate(flops=0, bytes_accessed=12 * rows * cols, transcendentals=0),
        name="home_apart",
    )(place, *backs, signal, gain, partial_out)


def exchange(values, axis, step):
    size = lax.axis_size(axis)
    return lax.ppermute(values, axis, [(i, i ^ step) for i in range(size)])


def spread(values):
    return lax.all_to_all(values, "seq", split_axis=0, concat_axis=0, tiled=True)


def after(value, *others):
    return lax.optimization_barrier((value, *others))[0]


def fast_body(signal, filters, skip_gain):
    blocks = lax.axis_size("seq")
    rows, width = signal.shape
    count = width // blocks // GROUP // 2
    cols = width // 2
    side = lax.axis_index("ch")
    place = jnp.stack([lax.axis_index("seq"), side]).astype(jnp.int32)
    gain = skip_gain.reshape(1, width)
    first = spread(turn_taps(signal, filters, blocks, (count, count)))
    second = spread(turn(signal, cols, cols).reshape(blocks, -1, rows))
    taps = first[:, count * GROUP :, :]
    own = lax.dynamic_slice_in_dim(taps, side * HALF, HALF, axis=2)
    other = exchange(lax.dynamic_slice_in_dim(taps, (1 - side) * HALF, HALF, axis=2), "ch", 1)
    (values,) = convolve(place, own, other, first, 0, count, False)
    back = spread(values).reshape(-1, rows)
    parts = convolve(place, own, other, second, count, count, True)
    parts = [exchange(part, "seq", j) if j else part for j, part in enumerate(parts)]
    out = home(back, signal, gain, 0, None)
    return home_apart(place, parts, signal, gain, out)


def angle_table(row_count, col_count, length, sign):
    row_index = jnp.arange(row_count, dtype=jnp.int32)[:, None]
    col_index = jnp.arange(col_count, dtype=jnp.int32)[None, :]
    phase = row_index * col_index % length
    angle = sign * 2.0 * math.pi / length * phase.astype(jnp.float32)
    return (jnp.cos(angle), jnp.sin(angle))


def complex_apply(form, table, real_part, imag_part):
    cosine, sine = table

    def product(matrix, values):
        return jnp.einsum(form, matrix, values, precision=HIGHEST_PRECISION)

    if imag_part is None:
        return (product(cosine, real_part), product(sine, real_part))
    return (
        product(cosine, real_part) - product(sine, imag_part),
        product(cosine, imag_part) + product(sine, real_part),
    )


def rotate(real_part, imag_part, cosine, sine):
    return (real_part * cosine - imag_part * sine, real_part * sine + imag_part * cosine)


def local_convolve(whole_sig, whole_taps, blocks, rows):
    width = whole_sig.shape[1]
    span = 2 * blocks * rows
    sig_blocks = whole_sig.reshape(blocks, rows, width)
    tap_blocks = whole_taps.reshape(blocks, rows, width)
    outer = angle_table(2 * blocks, blocks, 2 * blocks, -1.0)
    sig_real, sig_imag = complex_apply("kn,nbc->kbc", outer, sig_blocks, None)
    filt_real, filt_imag = complex_apply("kn,nbc->kbc", outer, tap_blocks, None)
    phase = (
        jnp.arange(2 * blocks, dtype=jnp.int32)[:, None]
        * jnp.arange(rows, dtype=jnp.int32)[None, :]
        % span
    )
    twist = 2.0 * math.pi / span * phase.astype(jnp.float32)
    twist_cos = jnp.cos(twist)[:, :, None]
    twist_sin = jnp.sin(twist)[:, :, None]
    sig_real, sig_imag = rotate(sig_real, sig_imag, twist_cos, -twist_sin)
    filt_real, filt_imag = rotate(filt_real, filt_imag, twist_cos, -twist_sin)
    inner = angle_table(rows, rows, rows, -1.0)
    sig_real, sig_imag = complex_apply("kn,bnc->bkc", inner, sig_real, sig_imag)
    filt_real, filt_imag = complex_apply("kn,bnc->bkc", inner, filt_real, filt_imag)
    prod_real, prod_imag = rotate(sig_real, sig_imag, filt_real, filt_imag)
    inverse_inner = angle_table(rows, rows, rows, 1.0)
    back_real, back_imag = complex_apply("nk,bkc->bnc", inverse_inner, prod_real, prod_imag)
    back_real, back_imag = rotate(back_real, back_imag, twist_cos, twist_sin)
    outer_back = angle_table(blocks, 2 * blocks, 2 * blocks, 1.0)
    values = jnp.einsum(
        "nk,kbc->nbc", outer_back[0], back_real, precision=HIGHEST_PRECISION
    ) - jnp.einsum("nk,kbc->nbc", outer_back[1], back_imag, precision=HIGHEST_PRECISION)
    return values.reshape(blocks * rows, width) / span


def spectral_body(signal, filters, skip_gain):
    blocks = lax.axis_size("seq")
    rows = signal.shape[0]
    taps = lax.all_to_all(filters, "ch", split_axis=1, concat_axis=0, tiled=True)
    local_groups = taps.shape[1]
    per_channel = jnp.broadcast_to(taps[:, :, None], (rows, local_groups, GROUP)).reshape(
        rows, local_groups * GROUP
    )
    whole_sig, whole_taps = (
        lax.all_to_all(signal, "seq", split_axis=1, concat_axis=0, tiled=True),
        lax.all_to_all(per_channel, "seq", split_axis=1, concat_axis=0, tiled=True),
    )
    values = local_convolve(whole_sig, whole_taps, blocks, rows)
    homed = lax.all_to_all(values, "seq", split_axis=0, concat_axis=1, tiled=True)
    return homed + skip_gain[None, :] * signal


def body(signal, filters, skip_gain):
    blocks = lax.axis_size("seq")
    rows, width = signal.shape
    lag_rows = filters.shape[0]
    fits = (
        blocks > 1
        and blocks & (blocks - 1) == 0
        and lax.axis_size("ch") == 2
        and width % (blocks * 2 * PAIR * GROUP) == 0
        and rows == 2 * HALF
        and lag_rows == HALF
    )
    if fits:
        return fast_body(signal, filters, skip_gain)
    return spectral_body(signal, filters, skip_gain)


def solution(mesh):
    placed = (P("seq", "ch"), P(("seq", "ch"), None), P("ch"))
    return jax.shard_map(
        body, mesh=mesh, in_specs=placed, out_specs=P("seq", "ch"), check_vma=False
    )
```

```python
import functools
import math

import jax
import jax.numpy as jnp
from jax import lax
from jax.experimental import pallas as pl
from jax.experimental.pallas import tpu as pltpu
from jax.sharding import PartitionSpec as P

GROUP = 16
HALF = 128
PAIR = 2
VMEM_BYTES = 60 * 1024 * 1024

HIGHEST_PRECISION = lax.Precision.HIGHEST


def split_halves(values):
    high = values.astype(jnp.bfloat16)
    low = (values - high.astype(jnp.float32)).astype(jnp.bfloat16)
    return high, low


def turned(in_ref):
    return in_ref[...].T


def turn_taps_kernel(counts, sig_ref, taps_ref, out_ref):
    blocks, _, rows = out_ref.shape
    per_chunk = sig_ref.shape[1] // blocks
    lag_rows, groups = taps_ref.shape
    out_ref[:, :per_chunk, :] = turned(sig_ref).reshape(blocks, per_chunk, rows)
    lines = turned(taps_ref)
    sides = rows // lag_rows
    for side in range(sides):
        row = per_chunk
        start = side * (groups // sides)
        for count in counts:
            for q in range(blocks):
                here = start + q * count
                at = slice(side * lag_rows, (side + 1) * lag_rows)
                out_ref[q, row : row + count, at] = lines[here : here + count]
            row += count
            start += blocks * count


def turn_taps(signal, filters, blocks, counts):
    rows, width = signal.shape
    cols = blocks * counts[0] * GROUP
    shape = (blocks, counts[0] * GROUP + sum(counts), rows)
    return pl.pallas_call(
        functools.partial(turn_taps_kernel, counts),
        grid=(1,),
        in_specs=[
            pl.BlockSpec((rows, cols), lambda i: (0, 0)),
            pl.BlockSpec(filters.shape, lambda i: (0, 0)),
        ],
        out_specs=pl.BlockSpec(shape, lambda i: (0, 0, 0)),
        out_shape=jax.ShapeDtypeStruct(shape, jnp.float32),
        compiler_params=pltpu.CompilerParams(vmem_limit_bytes=VMEM_BYTES),
        cost_estimate=pl.CostEstimate(flops=0, bytes_accessed=8 * rows * cols, transcendentals=0),
        name="turn_taps",
    )(signal, filters)


def turn_apart_kernel(place_ref, sig_ref, *rest):
    outs, hold_ref = rest[:-1], rest[-1]
    hold_ref[...] = turned(sig_ref).reshape(hold_ref.shape)
    for j, out_ref in enumerate(outs):
        out_ref[...] = hold_ref[place_ref[0] ^ j]


def turn_apart(place, signal, blocks):
    rows, width = signal.shape
    cols = width // 2
    shape = (cols // blocks, rows)
    return pl.pallas_call(
        turn_apart_kernel,
        grid=(1,),
        in_specs=[
            pl.BlockSpec(memory_space=pltpu.SMEM),
            pl.BlockSpec((rows, cols), lambda i: (0, 1)),
        ],
        out_specs=[pl.BlockSpec(shape, lambda i: (0, 0))] * blocks,
        out_shape=[jax.ShapeDtypeStruct(shape, jnp.float32)] * blocks,
        scratch_shapes=[pltpu.VMEM((blocks, *shape), jnp.float32)],
        compiler_params=pltpu.CompilerParams(vmem_limit_bytes=VMEM_BYTES),
        cost_estimate=pl.CostEstimate(flops=0, bytes_accessed=8 * rows * cols, transcendentals=0),
        name="turn_apart",
    )(place, signal)


def home_kernel(back_ref, sig_ref, gain_ref, *rest):
    rest[-1][...] = turned(back_ref) + gain_ref[...] * sig_ref[...]


def home(back, signal, gain, start, partial_out):
    rows, width = signal.shape
    cols = back.shape[0]
    step = math.gcd(start, cols)
    here = lambda i: (0, start // step + i)
    in_specs = [
        pl.BlockSpec((step, rows), lambda i: (i, 0)),
        pl.BlockSpec((rows, step), here),
        pl.BlockSpec((1, step), here),
    ]
    operands = [back, signal, gain]
    aliases = {}
    if partial_out is not None:
        in_specs.append(pl.BlockSpec(memory_space=pl.ANY))
        operands.append(partial_out)
        aliases = {3: 0}
    return pl.pallas_call(
        home_kernel,
        grid=(cols // step,),
        in_specs=in_specs,
        out_specs=pl.BlockSpec((rows, step), here),
        out_shape=jax.ShapeDtypeStruct((rows, width), jnp.float32),
        input_output_aliases=aliases,
        compiler_params=pltpu.CompilerParams(vmem_limit_bytes=VMEM_BYTES),
        cost_estimate=pl.CostEstimate(flops=0, bytes_accessed=12 * rows * cols, transcendentals=0),
        name="home",
    )(*operands)


def shifted_taps(side, group, own_ref, other_ref, high_ref, low_ref):
    blocks = own_ref.shape[0]

    def line(ref, q):
        return jnp.broadcast_to(ref[q, pl.ds(group, 1), :], (8, HALF))

    lines = []
    for q in range(blocks):
        own, other = line(own_ref, q), line(other_ref, q)
        lines += [jnp.where(side == 0, own, other), jnp.where(side == 0, other, own)]
    blank = jnp.zeros((8, HALF), jnp.float32)
    strip = jnp.concatenate([blank] + lines + [blank], axis=1)
    strip = pltpu.roll(strip, 0, 1, stride=1, stride_axis=0)
    for p in range(HALF // 16):
        pair = jnp.concatenate(
            [pltpu.roll(strip, 16 * p, 1) if p else strip, pltpu.roll(strip, 16 * p + 8, 1)], axis=0
        )
        high, low = split_halves(pair)
        high_ref[16 * p : 16 * p + 16, :] = high
        low_ref[16 * p : 16 * p + 16, :] = low


def causal_sums(signal, high_ref, low_ref, sum_ref):
    rows = signal.shape[1]
    blocks = signal.shape[0] // GROUP
    sig_high, sig_low = split_halves(signal)

    def window(ref, lag_block):
        start = lag_block * rows
        return jnp.concatenate(
            [ref[:, start + HALF * k : start + HALF * k + rows] for k in (1, 0)], axis=0
        )

    for d in range(blocks):
        n = (blocks - d) * GROUP
        taps_high, taps_low = window(high_ref, d), window(low_ref, d)
        both = jnp.concatenate([sig_high[:n], sig_low[:n]], axis=0)
        part = jnp.dot(both, taps_high, preferred_element_type=jnp.float32)
        term = part[:n] + part[n:]
        term = term + jnp.dot(sig_high[:n], taps_low, preferred_element_type=jnp.float32)
        if d == 0:
            sum_ref[...] = term
        else:
            sum_ref[d * GROUP :, :] += term


def conv_kernel(first, place_ref, own_ref, other_ref, sig_ref, *rest):
    out_ref, scratch = rest[0], rest[-3 * PAIR :]
    blocks, _, rows = sig_ref.shape
    for u in range(PAIR):
        group = first + PAIR * pl.program_id(0) + u
        shifted_taps(place_ref[1], group, own_ref, other_ref, scratch[3 * u], scratch[3 * u + 1])
    for u in range(PAIR):
        high_ref, low_ref, sum_ref = scratch[3 * u : 3 * u + 3]
        at = slice(u * GROUP, (u + 1) * GROUP)
        causal_sums(sig_ref[:, at, :].reshape(blocks * GROUP, rows), high_ref, low_ref, sum_ref)
        out_ref[:, at, :] = sum_ref[...].reshape(blocks, GROUP, rows)


def conv_apart_kernel(first, blocks, place_ref, own_ref, other_ref, *rest):
    sigs, outs, hold_ref = rest[:blocks], rest[blocks : 2 * blocks], rest[2 * blocks]
    scratch = rest[2 * blocks + 1 :]
    rows = hold_ref.shape[2]
    me, side = place_ref[0], place_ref[1]
    for j, sig_ref in enumerate(sigs):
        hold_ref[me ^ j] = sig_ref[...]
    for u in range(PAIR):
        group = first + PAIR * pl.program_id(0) + u
        shifted_taps(side, group, own_ref, other_ref, scratch[3 * u], scratch[3 * u + 1])
    for u in range(PAIR):
        high_ref, low_ref, sum_ref = scratch[3 * u : 3 * u + 3]
        at = slice(u * GROUP, (u + 1) * GROUP)
        causal_sums(hold_ref[:, at, :].reshape(blocks * GROUP, rows), high_ref, low_ref, sum_ref)
        for j in range(blocks):
            row = pl.multiple_of((me ^ j) * GROUP, GROUP)
            outs[j][at, :] = sum_ref[pl.ds(row, GROUP), :]


def conv_scratch(blocks, rows):
    lanes = blocks * rows + 2 * HALF
    return [
        pltpu.VMEM((HALF, lanes), jnp.bfloat16),
        pltpu.VMEM((HALF, lanes), jnp.bfloat16),
        pltpu.VMEM((blocks * GROUP, rows), jnp.float32),
    ] * PAIR


def conv_cost(blocks, groups, rows):
    return pl.CostEstimate(
        flops=3 * groups * GROUP * rows * rows * blocks * (blocks + 1),
        bytes_accessed=8 * blocks * groups * GROUP * rows,
        transcendentals=0,
    )


def convolve(place, own, other, arrived, first, groups):
    blocks, _, rows = arrived.shape
    spec = pl.BlockSpec((blocks, PAIR * GROUP, rows), lambda g: (0, g, 0))
    taps_spec = pl.BlockSpec(own.shape, lambda g: (0, 0, 0))
    return pl.pallas_call(
        functools.partial(conv_kernel, first),
        grid=(groups // PAIR,),
        in_specs=[pl.BlockSpec(memory_space=pltpu.SMEM), taps_spec, taps_spec, spec],
        out_specs=spec,
        out_shape=jax.ShapeDtypeStruct((blocks, groups * GROUP, rows), jnp.float32),
        scratch_shapes=conv_scratch(blocks, rows),
        compiler_params=pltpu.CompilerParams(vmem_limit_bytes=VMEM_BYTES),
        cost_estimate=conv_cost(blocks, groups, rows),
        name="convolve",
    )(place, own, other, arrived)


def convolve_apart(place, own, other, parts, first):
    blocks = len(parts)
    deep, rows = parts[0].shape
    groups = deep // GROUP
    taps_spec = pl.BlockSpec(own.shape, lambda g: (0, 0, 0))
    pieces = [pl.BlockSpec((PAIR * GROUP, rows), lambda g: (g, 0))] * blocks
    return pl.pallas_call(
        functools.partial(conv_apart_kernel, first, blocks),
        grid=(groups // PAIR,),
        in_specs=[pl.BlockSpec(memory_space=pltpu.SMEM), taps_spec, taps_spec] + pieces,
        out_specs=pieces,
        out_shape=[jax.ShapeDtypeStruct((deep, rows), jnp.float32)] * blocks,
        scratch_shapes=[pltpu.VMEM((blocks, PAIR * GROUP, rows), jnp.float32)]
        + conv_scratch(blocks, rows),
        compiler_params=pltpu.CompilerParams(vmem_limit_bytes=VMEM_BYTES),
        cost_estimate=conv_cost(blocks, groups, rows),
        name="convolve_apart",
    )(place, own, other, *parts)


def home_apart_kernel(place_ref, *rest):
    back_refs, (sig_ref, gain_ref, _, out_ref, hold_ref) = rest[:-5], rest[-5:]
    me = place_ref[0]
    for j, back_ref in enumerate(back_refs):
        hold_ref[me ^ j] = back_ref[...]
    values = hold_ref[...].reshape(sig_ref.shape[1], sig_ref.shape[0])
    out_ref[...] = values.T + gain_ref[...] * sig_ref[...]


def home_apart(place, backs, signal, gain, partial_out):
    rows, width = signal.shape
    blocks, per_chunk = len(backs), backs[0].shape[0]
    cols = blocks * per_chunk
    here = lambda i: (0, 1)
    return pl.pallas_call(
        home_apart_kernel,
        grid=(1,),
        in_specs=[pl.BlockSpec(memory_space=pltpu.SMEM)]
        + [pl.BlockSpec((per_chunk, rows), lambda i: (0, 0))] * blocks
        + [pl.BlockSpec((rows, cols), here), pl.BlockSpec((1, cols), here)]
        + [pl.BlockSpec(memory_space=pl.ANY)],
        out_specs=pl.BlockSpec((rows, cols), here),
        out_shape=jax.ShapeDtypeStruct((rows, width), jnp.float32),
        input_output_aliases={blocks + 3: 0},
        scratch_shapes=[pltpu.VMEM((blocks, per_chunk, rows), jnp.float32)],
        compiler_params=pltpu.CompilerParams(vmem_limit_bytes=VMEM_BYTES),
        cost_estimate=pl.CostEstimate(flops=0, bytes_accessed=12 * rows * cols, transcendentals=0),
        name="home_apart",
    )(place, *backs, signal, gain, partial_out)


def exchange(values, axis, step):
    size = lax.axis_size(axis)
    return lax.ppermute(values, axis, [(i, i ^ step) for i in range(size)])


def spread(values):
    return lax.all_to_all(values, "seq", split_axis=0, concat_axis=0, tiled=True)


def after(value, *others):
    return lax.optimization_barrier((value, *others))[0]


def scatter(parts):
    return [exchange(part, "seq", j) if j else part for j, part in enumerate(parts)]


def fast_body(signal, filters, skip_gain):
    blocks = lax.axis_size("seq")
    rows, width = signal.shape
    count = width // blocks // GROUP // 2
    side = lax.axis_index("ch")
    place = jnp.stack([lax.axis_index("seq"), side]).astype(jnp.int32)
    gain = skip_gain.reshape(1, width)
    first = spread(turn_taps(signal, filters, blocks, (count, count)))
    parts = scatter(turn_apart(place, signal, blocks))
    first = after(first, *parts[1:8])
    taps = first[:, count * GROUP :, :]
    own = lax.dynamic_slice_in_dim(taps, side * HALF, HALF, axis=2)
    other = exchange(lax.dynamic_slice_in_dim(taps, (1 - side) * HALF, HALF, axis=2), "ch", 1)
    values = convolve(place, own, other, first, 0, count)
    values = after(values, *parts[8:])
    back = spread(values).reshape(-1, rows)
    parts = scatter(convolve_apart(place, own, other, parts, count))
    out = home(back, signal, gain, 0, None)
    return home_apart(place, parts, signal, gain, out)


def angle_table(row_count, col_count, length, sign):
    row_index = jnp.arange(row_count, dtype=jnp.int32)[:, None]
    col_index = jnp.arange(col_count, dtype=jnp.int32)[None, :]
    phase = row_index * col_index % length
    angle = sign * 2.0 * math.pi / length * phase.astype(jnp.float32)
    return (jnp.cos(angle), jnp.sin(angle))


def complex_apply(form, table, real_part, imag_part):
    cosine, sine = table

    def product(matrix, values):
        return jnp.einsum(form, matrix, values, precision=HIGHEST_PRECISION)

    if imag_part is None:
        return (product(cosine, real_part), product(sine, real_part))
    return (
        product(cosine, real_part) - product(sine, imag_part),
        product(cosine, imag_part) + product(sine, real_part),
    )


def rotate(real_part, imag_part, cosine, sine):
    return (real_part * cosine - imag_part * sine, real_part * sine + imag_part * cosine)


def local_convolve(whole_sig, whole_taps, blocks, rows):
    width = whole_sig.shape[1]
    span = 2 * blocks * rows
    sig_blocks = whole_sig.reshape(blocks, rows, width)
    tap_blocks = whole_taps.reshape(blocks, rows, width)
    outer = angle_table(2 * blocks, blocks, 2 * blocks, -1.0)
    sig_real, sig_imag = complex_apply("kn,nbc->kbc", outer, sig_blocks, None)
    filt_real, filt_imag = complex_apply("kn,nbc->kbc", outer, tap_blocks, None)
    phase = (
        jnp.arange(2 * blocks, dtype=jnp.int32)[:, None]
        * jnp.arange(rows, dtype=jnp.int32)[None, :]
        % span
    )
    twist = 2.0 * math.pi / span * phase.astype(jnp.float32)
    twist_cos = jnp.cos(twist)[:, :, None]
    twist_sin = jnp.sin(twist)[:, :, None]
    sig_real, sig_imag = rotate(sig_real, sig_imag, twist_cos, -twist_sin)
    filt_real, filt_imag = rotate(filt_real, filt_imag, twist_cos, -twist_sin)
    inner = angle_table(rows, rows, rows, -1.0)
    sig_real, sig_imag = complex_apply("kn,bnc->bkc", inner, sig_real, sig_imag)
    filt_real, filt_imag = complex_apply("kn,bnc->bkc", inner, filt_real, filt_imag)
    prod_real, prod_imag = rotate(sig_real, sig_imag, filt_real, filt_imag)
    inverse_inner = angle_table(rows, rows, rows, 1.0)
    back_real, back_imag = complex_apply("nk,bkc->bnc", inverse_inner, prod_real, prod_imag)
    back_real, back_imag = rotate(back_real, back_imag, twist_cos, twist_sin)
    outer_back = angle_table(blocks, 2 * blocks, 2 * blocks, 1.0)
    values = jnp.einsum(
        "nk,kbc->nbc", outer_back[0], back_real, precision=HIGHEST_PRECISION
    ) - jnp.einsum("nk,kbc->nbc", outer_back[1], back_imag, precision=HIGHEST_PRECISION)
    return values.reshape(blocks * rows, width) / span


def spectral_body(signal, filters, skip_gain):
    blocks = lax.axis_size("seq")
    rows = signal.shape[0]
    taps = lax.all_to_all(filters, "ch", split_axis=1, concat_axis=0, tiled=True)
    local_groups = taps.shape[1]
    per_channel = jnp.broadcast_to(taps[:, :, None], (rows, local_groups, GROUP)).reshape(
        rows, local_groups * GROUP
    )
    whole_sig, whole_taps = (
        lax.all_to_all(signal, "seq", split_axis=1, concat_axis=0, tiled=True),
        lax.all_to_all(per_channel, "seq", split_axis=1, concat_axis=0, tiled=True),
    )
    values = local_convolve(whole_sig, whole_taps, blocks, rows)
    homed = lax.all_to_all(values, "seq", split_axis=0, concat_axis=1, tiled=True)
    return homed + skip_gain[None, :] * signal


def body(signal, filters, skip_gain):
    blocks = lax.axis_size("seq")
    rows, width = signal.shape
    lag_rows = filters.shape[0]
    fits = (
        blocks > 1
        and blocks & (blocks - 1) == 0
        and lax.axis_size("ch") == 2
        and width % (blocks * 2 * PAIR * GROUP) == 0
        and rows == 2 * HALF
        and lag_rows == HALF
    )
    if fits:
        return fast_body(signal, filters, skip_gain)
    return spectral_body(signal, filters, skip_gain)


def solution(mesh):
    placed = (P("seq", "ch"), P(("seq", "ch"), None), P("ch"))
    return jax.shard_map(
        body, mesh=mesh, in_specs=placed, out_specs=P("seq", "ch"), check_vma=False
    )
```

```python
import functools
import math

import jax
import jax.numpy as jnp
from jax import lax
from jax.experimental import pallas as pl
from jax.experimental.pallas import tpu as pltpu
from jax.sharding import PartitionSpec as P

GROUP = 16
HALF = 128
PAIR = 2
CORES = 2
VMEM_BYTES = 60 * 1024 * 1024

HIGHEST_PRECISION = lax.Precision.HIGHEST


def split_halves(values):
    high = values.astype(jnp.bfloat16)
    low = (values - high.astype(jnp.float32)).astype(jnp.bfloat16)
    return high, low


def turned(in_ref):
    return in_ref[...].T


def turn_taps_kernel(counts, sig_ref, taps_ref, out_ref):
    blocks, _, rows = out_ref.shape
    per_chunk = sig_ref.shape[1] // blocks
    lag_rows, groups = taps_ref.shape
    out_ref[:, :per_chunk, :] = turned(sig_ref).reshape(blocks, per_chunk, rows)
    lines = turned(taps_ref)
    sides = rows // lag_rows
    for side in range(sides):
        row = per_chunk
        start = side * (groups // sides)
        for count in counts:
            for q in range(blocks):
                here = start + q * count
                at = slice(side * lag_rows, (side + 1) * lag_rows)
                out_ref[q, row : row + count, at] = lines[here : here + count]
            row += count
            start += blocks * count


def turn_taps(signal, filters, blocks, counts):
    rows, width = signal.shape
    cols = blocks * counts[0] * GROUP
    shape = (blocks, counts[0] * GROUP + sum(counts), rows)
    return pl.pallas_call(
        functools.partial(turn_taps_kernel, counts),
        grid=(1,),
        in_specs=[
            pl.BlockSpec((rows, cols), lambda i: (0, 0)),
            pl.BlockSpec(filters.shape, lambda i: (0, 0)),
        ],
        out_specs=pl.BlockSpec(shape, lambda i: (0, 0, 0)),
        out_shape=jax.ShapeDtypeStruct(shape, jnp.float32),
        compiler_params=pltpu.CompilerParams(vmem_limit_bytes=VMEM_BYTES),
        cost_estimate=pl.CostEstimate(flops=0, bytes_accessed=8 * rows * cols, transcendentals=0),
        name="turn_taps",
    )(signal, filters)


def turn_apart_kernel(place_ref, sig_ref, *rest):
    outs, hold_ref = rest[:-1], rest[-1]
    hold_ref[...] = turned(sig_ref).reshape(hold_ref.shape)
    for j, out_ref in enumerate(outs):
        for e in range(CORES):
            out_ref[e] = hold_ref[place_ref[0] ^ (CORES * j + e)]


def turn_apart(place, signal, blocks):
    rows, width = signal.shape
    cols = width // 2
    shape = (cols // blocks, rows)
    pairs = blocks // CORES
    return pl.pallas_call(
        turn_apart_kernel,
        grid=(1,),
        in_specs=[
            pl.BlockSpec(memory_space=pltpu.SMEM),
            pl.BlockSpec((rows, cols), lambda i: (0, 1)),
        ],
        out_specs=[pl.BlockSpec((CORES, *shape), lambda i: (0, 0, 0))] * pairs,
        out_shape=[jax.ShapeDtypeStruct((CORES, *shape), jnp.float32)] * pairs,
        scratch_shapes=[pltpu.VMEM((blocks, *shape), jnp.float32)],
        compiler_params=pltpu.CompilerParams(vmem_limit_bytes=VMEM_BYTES),
        cost_estimate=pl.CostEstimate(flops=0, bytes_accessed=8 * rows * cols, transcendentals=0),
        name="turn_apart",
    )(place, signal)


def home_kernel(back_ref, sig_ref, gain_ref, *rest):
    rest[-1][...] = turned(back_ref) + gain_ref[...] * sig_ref[...]


def home(back, signal, gain, start, partial_out):
    rows, width = signal.shape
    cols = back.shape[0]
    step = math.gcd(start, cols)
    here = lambda i: (0, start // step + i)
    in_specs = [
        pl.BlockSpec((step, rows), lambda i: (i, 0)),
        pl.BlockSpec((rows, step), here),
        pl.BlockSpec((1, step), here),
    ]
    operands = [back, signal, gain]
    aliases = {}
    if partial_out is not None:
        in_specs.append(pl.BlockSpec(memory_space=pl.ANY))
        operands.append(partial_out)
        aliases = {3: 0}
    return pl.pallas_call(
        home_kernel,
        grid=(cols // step,),
        in_specs=in_specs,
        out_specs=pl.BlockSpec((rows, step), here),
        out_shape=jax.ShapeDtypeStruct((rows, width), jnp.float32),
        input_output_aliases=aliases,
        compiler_params=pltpu.CompilerParams(vmem_limit_bytes=VMEM_BYTES),
        cost_estimate=pl.CostEstimate(flops=0, bytes_accessed=12 * rows * cols, transcendentals=0),
        name="home",
    )(*operands)


def shifted_taps(side, group, own_ref, other_ref, high_ref, low_ref):
    blocks = own_ref.shape[0]

    def line(ref, q):
        return jnp.broadcast_to(ref[q, pl.ds(group, 1), :], (8, HALF))

    lines = []
    for q in range(blocks):
        own, other = line(own_ref, q), line(other_ref, q)
        lines += [jnp.where(side == 0, own, other), jnp.where(side == 0, other, own)]
    blank = jnp.zeros((8, HALF), jnp.float32)
    strip = jnp.concatenate([blank] + lines + [blank], axis=1)
    strip = pltpu.roll(strip, 0, 1, stride=1, stride_axis=0)
    for p in range(HALF // 16):
        pair = jnp.concatenate(
            [pltpu.roll(strip, 16 * p, 1) if p else strip, pltpu.roll(strip, 16 * p + 8, 1)], axis=0
        )
        high, low = split_halves(pair)
        high_ref[16 * p : 16 * p + 16, :] = high
        low_ref[16 * p : 16 * p + 16, :] = low


def causal_sums(signal, high_ref, low_ref, sum_ref):
    rows = signal.shape[1]
    blocks = signal.shape[0] // GROUP
    sig_high, sig_low = split_halves(signal)

    def window(ref, lag_block):
        start = lag_block * rows
        return jnp.concatenate(
            [ref[:, start + HALF * k : start + HALF * k + rows] for k in (1, 0)], axis=0
        )

    for d in range(blocks):
        n = (blocks - d) * GROUP
        taps_high, taps_low = window(high_ref, d), window(low_ref, d)
        both = jnp.concatenate([sig_high[:n], sig_low[:n]], axis=0)
        part = jnp.dot(both, taps_high, preferred_element_type=jnp.float32)
        term = part[:n] + part[n:]
        term = term + jnp.dot(sig_high[:n], taps_low, preferred_element_type=jnp.float32)
        if d == 0:
            sum_ref[...] = term
        else:
            sum_ref[d * GROUP :, :] += term


def conv_kernel(first, place_ref, own_ref, other_ref, sig_ref, *rest):
    out_ref, scratch = rest[0], rest[-3 * PAIR :]
    blocks, _, rows = sig_ref.shape
    for u in range(PAIR):
        group = first + PAIR * pl.program_id(0) + u
        shifted_taps(place_ref[1], group, own_ref, other_ref, scratch[3 * u], scratch[3 * u + 1])
    for u in range(PAIR):
        high_ref, low_ref, sum_ref = scratch[3 * u : 3 * u + 3]
        at = slice(u * GROUP, (u + 1) * GROUP)
        causal_sums(sig_ref[:, at, :].reshape(blocks * GROUP, rows), high_ref, low_ref, sum_ref)
        out_ref[:, at, :] = sum_ref[...].reshape(blocks, GROUP, rows)


def conv_apart_kernel(first, pairs, place_ref, own_ref, other_ref, passed_ref, *rest):
    blocks = CORES * pairs
    sigs, outs, hold_ref = rest[:pairs], rest[pairs : pairs + blocks], rest[pairs + blocks]
    scratch = rest[pairs + blocks + 1 :]
    rows = hold_ref.shape[2]
    me, side = place_ref[0], place_ref[1]
    for j, sig_ref in enumerate(sigs):
        hold_ref[me ^ (CORES * j)] = sig_ref[0]
        hold_ref[me ^ (CORES * j + 1)] = passed_ref[j]
    for u in range(PAIR):
        group = first + PAIR * pl.program_id(0) + u
        shifted_taps(side, group, own_ref, other_ref, scratch[3 * u], scratch[3 * u + 1])
    for u in range(PAIR):
        high_ref, low_ref, sum_ref = scratch[3 * u : 3 * u + 3]
        at = slice(u * GROUP, (u + 1) * GROUP)
        causal_sums(hold_ref[:, at, :].reshape(blocks * GROUP, rows), high_ref, low_ref, sum_ref)
        for j in range(blocks):
            row = pl.multiple_of((me ^ j) * GROUP, GROUP)
            outs[j][at, :] = sum_ref[pl.ds(row, GROUP), :]


def conv_scratch(blocks, rows):
    lanes = blocks * rows + 2 * HALF
    return [
        pltpu.VMEM((HALF, lanes), jnp.bfloat16),
        pltpu.VMEM((HALF, lanes), jnp.bfloat16),
        pltpu.VMEM((blocks * GROUP, rows), jnp.float32),
    ] * PAIR


def conv_cost(blocks, groups, rows):
    return pl.CostEstimate(
        flops=3 * groups * GROUP * rows * rows * blocks * (blocks + 1),
        bytes_accessed=8 * blocks * groups * GROUP * rows,
        transcendentals=0,
    )


def convolve(place, own, other, arrived, first, groups):
    blocks, _, rows = arrived.shape
    spec = pl.BlockSpec((blocks, PAIR * GROUP, rows), lambda g: (0, g, 0))
    taps_spec = pl.BlockSpec(own.shape, lambda g: (0, 0, 0))
    return pl.pallas_call(
        functools.partial(conv_kernel, first),
        grid=(groups // PAIR,),
        in_specs=[pl.BlockSpec(memory_space=pltpu.SMEM), taps_spec, taps_spec, spec],
        out_specs=spec,
        out_shape=jax.ShapeDtypeStruct((blocks, groups * GROUP, rows), jnp.float32),
        scratch_shapes=conv_scratch(blocks, rows),
        compiler_params=pltpu.CompilerParams(vmem_limit_bytes=VMEM_BYTES),
        cost_estimate=conv_cost(blocks, groups, rows),
        name="convolve",
    )(place, own, other, arrived)


def convolve_apart(place, own, other, passed, parts, first):
    pairs, deep, rows = passed.shape
    blocks = CORES * pairs
    groups = deep // GROUP
    taps_spec = pl.BlockSpec(own.shape, lambda g: (0, 0, 0))
    return pl.pallas_call(
        functools.partial(conv_apart_kernel, first, pairs),
        grid=(groups // PAIR,),
        in_specs=[
            pl.BlockSpec(memory_space=pltpu.SMEM),
            taps_spec,
            taps_spec,
            pl.BlockSpec((pairs, PAIR * GROUP, rows), lambda g: (0, g, 0)),
        ]
        + [pl.BlockSpec((1, PAIR * GROUP, rows), lambda g: (0, g, 0))] * pairs,
        out_specs=[pl.BlockSpec((PAIR * GROUP, rows), lambda g: (g, 0))] * blocks,
        out_shape=[jax.ShapeDtypeStruct((deep, rows), jnp.float32)] * blocks,
        scratch_shapes=[pltpu.VMEM((blocks, PAIR * GROUP, rows), jnp.float32)]
        + conv_scratch(blocks, rows),
        compiler_params=pltpu.CompilerParams(vmem_limit_bytes=VMEM_BYTES),
        cost_estimate=conv_cost(blocks, groups, rows),
        name="convolve_apart",
    )(place, own, other, passed, *parts)


def home_apart_kernel(place_ref, *rest):
    back_refs, (sig_ref, gain_ref, _, out_ref, hold_ref) = rest[:-5], rest[-5:]
    me = place_ref[0]
    for j, back_ref in enumerate(back_refs):
        hold_ref[me ^ j] = back_ref[...]
    values = hold_ref[...].reshape(sig_ref.shape[1], sig_ref.shape[0])
    out_ref[...] = values.T + gain_ref[...] * sig_ref[...]


def home_apart(place, backs, signal, gain, partial_out):
    rows, width = signal.shape
    blocks, per_chunk = len(backs), backs[0].shape[0]
    cols = blocks * per_chunk
    here = lambda i: (0, 1)
    return pl.pallas_call(
        home_apart_kernel,
        grid=(1,),
        in_specs=[pl.BlockSpec(memory_space=pltpu.SMEM)]
        + [pl.BlockSpec((per_chunk, rows), lambda i: (0, 0))] * blocks
        + [pl.BlockSpec((rows, cols), here), pl.BlockSpec((1, cols), here)]
        + [pl.BlockSpec(memory_space=pl.ANY)],
        out_specs=pl.BlockSpec((rows, cols), here),
        out_shape=jax.ShapeDtypeStruct((rows, width), jnp.float32),
        input_output_aliases={blocks + 3: 0},
        scratch_shapes=[pltpu.VMEM((blocks, per_chunk, rows), jnp.float32)],
        compiler_params=pltpu.CompilerParams(vmem_limit_bytes=VMEM_BYTES),
        cost_estimate=pl.CostEstimate(flops=0, bytes_accessed=12 * rows * cols, transcendentals=0),
        name="home_apart",
    )(place, *backs, signal, gain, partial_out)


def exchange(values, axis, step):
    size = lax.axis_size(axis)
    return lax.ppermute(values, axis, [(i, i ^ step) for i in range(size)])


def spread(values):
    return lax.all_to_all(values, "seq", split_axis=0, concat_axis=0, tiled=True)


def after(value, *others):
    return lax.optimization_barrier((value, *others))[0]


def scatter(parts, stride):
    return [exchange(part, "seq", stride * j) if j else part for j, part in enumerate(parts)]


def fast_body(signal, filters, skip_gain):
    blocks = lax.axis_size("seq")
    rows, width = signal.shape
    count = width // blocks // GROUP // 2
    side = lax.axis_index("ch")
    place = jnp.stack([lax.axis_index("seq"), side]).astype(jnp.int32)
    gain = skip_gain.reshape(1, width)
    first = spread(turn_taps(signal, filters, blocks, (count, count)))
    raw = turn_apart(place, signal, blocks)
    parts = scatter(raw[:6], CORES)
    first = after(first, *parts[1:4])
    parts += [exchange(after(part, first), "seq", CORES * (6 + j)) for j, part in enumerate(raw[6:])]
    taps = first[:, count * GROUP :, :]
    own = lax.dynamic_slice_in_dim(taps, side * HALF, HALF, axis=2)
    other = exchange(lax.dynamic_slice_in_dim(taps, (1 - side) * HALF, HALF, axis=2), "ch", 1)
    values = convolve(place, own, other, first, 0, count)
    values = after(values, *parts[4:8])
    back = spread(values).reshape(-1, rows)
    passed = exchange(jnp.stack([part[1] for part in parts]), "seq", 1)
    parts = scatter(convolve_apart(place, own, other, passed, parts, count), 1)
    out = home(back, signal, gain, 0, None)
    return home_apart(place, parts, signal, gain, out)


def angle_table(row_count, col_count, length, sign):
    row_index = jnp.arange(row_count, dtype=jnp.int32)[:, None]
    col_index = jnp.arange(col_count, dtype=jnp.int32)[None, :]
    phase = row_index * col_index % length
    angle = sign * 2.0 * math.pi / length * phase.astype(jnp.float32)
    return (jnp.cos(angle), jnp.sin(angle))


def complex_apply(form, table, real_part, imag_part):
    cosine, sine = table

    def product(matrix, values):
        return jnp.einsum(form, matrix, values, precision=HIGHEST_PRECISION)

    if imag_part is None:
        return (product(cosine, real_part), product(sine, real_part))
    return (
        product(cosine, real_part) - product(sine, imag_part),
        product(cosine, imag_part) + product(sine, real_part),
    )


def rotate(real_part, imag_part, cosine, sine):
    return (real_part * cosine - imag_part * sine, real_part * sine + imag_part * cosine)


def local_convolve(whole_sig, whole_taps, blocks, rows):
    width = whole_sig.shape[1]
    span = 2 * blocks * rows
    sig_blocks = whole_sig.reshape(blocks, rows, width)
    tap_blocks = whole_taps.reshape(blocks, rows, width)
    outer = angle_table(2 * blocks, blocks, 2 * blocks, -1.0)
    sig_real, sig_imag = complex_apply("kn,nbc->kbc", outer, sig_blocks, None)
    filt_real, filt_imag = complex_apply("kn,nbc->kbc", outer, tap_blocks, None)
    phase = (
        jnp.arange(2 * blocks, dtype=jnp.int32)[:, None]
        * jnp.arange(rows, dtype=jnp.int32)[None, :]
        % span
    )
    twist = 2.0 * math.pi / span * phase.astype(jnp.float32)
    twist_cos = jnp.cos(twist)[:, :, None]
    twist_sin = jnp.sin(twist)[:, :, None]
    sig_real, sig_imag = rotate(sig_real, sig_imag, twist_cos, -twist_sin)
    filt_real, filt_imag = rotate(filt_real, filt_imag, twist_cos, -twist_sin)
    inner = angle_table(rows, rows, rows, -1.0)
    sig_real, sig_imag = complex_apply("kn,bnc->bkc", inner, sig_real, sig_imag)
    filt_real, filt_imag = complex_apply("kn,bnc->bkc", inner, filt_real, filt_imag)
    prod_real, prod_imag = rotate(sig_real, sig_imag, filt_real, filt_imag)
    inverse_inner = angle_table(rows, rows, rows, 1.0)
    back_real, back_imag = complex_apply("nk,bkc->bnc", inverse_inner, prod_real, prod_imag)
    back_real, back_imag = rotate(back_real, back_imag, twist_cos, twist_sin)
    outer_back = angle_table(blocks, 2 * blocks, 2 * blocks, 1.0)
    values = jnp.einsum(
        "nk,kbc->nbc", outer_back[0], back_real, precision=HIGHEST_PRECISION
    ) - jnp.einsum("nk,kbc->nbc", outer_back[1], back_imag, precision=HIGHEST_PRECISION)
    return values.reshape(blocks * rows, width) / span


def spectral_body(signal, filters, skip_gain):
    blocks = lax.axis_size("seq")
    rows = signal.shape[0]
    taps = lax.all_to_all(filters, "ch", split_axis=1, concat_axis=0, tiled=True)
    local_groups = taps.shape[1]
    per_channel = jnp.broadcast_to(taps[:, :, None], (rows, local_groups, GROUP)).reshape(
        rows, local_groups * GROUP
    )
    whole_sig, whole_taps = (
        lax.all_to_all(signal, "seq", split_axis=1, concat_axis=0, tiled=True),
        lax.all_to_all(per_channel, "seq", split_axis=1, concat_axis=0, tiled=True),
    )
    values = local_convolve(whole_sig, whole_taps, blocks, rows)
    homed = lax.all_to_all(values, "seq", split_axis=0, concat_axis=1, tiled=True)
    return homed + skip_gain[None, :] * signal


def body(signal, filters, skip_gain):
    blocks = lax.axis_size("seq")
    rows, width = signal.shape
    lag_rows = filters.shape[0]
    fits = (
        blocks >= 2 * CORES
        and blocks & (blocks - 1) == 0
        and lax.axis_size("ch") == 2
        and width % (blocks * 2 * PAIR * GROUP) == 0
        and rows == 2 * HALF
        and lag_rows == HALF
    )
    if fits:
        return fast_body(signal, filters, skip_gain)
    return spectral_body(signal, filters, skip_gain)


def solution(mesh):
    placed = (P("seq", "ch"), P(("seq", "ch"), None), P("ch"))
    return jax.shard_map(
        body, mesh=mesh, in_specs=placed, out_specs=P("seq", "ch"), check_vma=False
    )
```

```python
import functools
import math

import jax
import jax.numpy as jnp
from jax import lax
from jax.experimental import pallas as pl
from jax.experimental.pallas import tpu as pltpu
from jax.sharding import PartitionSpec as P

GROUP = 16
HALF = 128
PAIR = 2
CORES = 2
VMEM_BYTES = 60 * 1024 * 1024

HIGHEST_PRECISION = lax.Precision.HIGHEST


def split_halves(values):
    high = values.astype(jnp.bfloat16)
    low = (values - high.astype(jnp.float32)).astype(jnp.bfloat16)
    return high, low


def turned(in_ref):
    return in_ref[...].T


def turn_taps_kernel(counts, sig_ref, taps_ref, out_ref):
    blocks, _, rows = out_ref.shape
    per_chunk = sig_ref.shape[1] // blocks
    lag_rows, groups = taps_ref.shape
    out_ref[:, :per_chunk, :] = turned(sig_ref).reshape(blocks, per_chunk, rows)
    lines = turned(taps_ref)
    sides = rows // lag_rows
    for side in range(sides):
        row = per_chunk
        start = side * (groups // sides)
        for count in counts:
            for q in range(blocks):
                here = start + q * count
                at = slice(side * lag_rows, (side + 1) * lag_rows)
                out_ref[q, row : row + count, at] = lines[here : here + count]
            row += count
            start += blocks * count


def turn_taps(signal, filters, blocks, counts):
    rows, width = signal.shape
    cols = blocks * counts[0] * GROUP
    shape = (blocks, counts[0] * GROUP + sum(counts), rows)
    return pl.pallas_call(
        functools.partial(turn_taps_kernel, counts),
        grid=(1,),
        in_specs=[
            pl.BlockSpec((rows, cols), lambda i: (0, 0)),
            pl.BlockSpec(filters.shape, lambda i: (0, 0)),
        ],
        out_specs=pl.BlockSpec(shape, lambda i: (0, 0, 0)),
        out_shape=jax.ShapeDtypeStruct(shape, jnp.float32),
        compiler_params=pltpu.CompilerParams(vmem_limit_bytes=VMEM_BYTES),
        cost_estimate=pl.CostEstimate(flops=0, bytes_accessed=8 * rows * cols, transcendentals=0),
        name="turn_taps",
    )(signal, filters)


def turn_apart_kernel(place_ref, sig_ref, *rest):
    outs, hold_ref = rest[:-1], rest[-1]
    hold_ref[...] = turned(sig_ref).reshape(hold_ref.shape)
    for j, out_ref in enumerate(outs):
        for e in range(CORES):
            out_ref[e] = hold_ref[place_ref[0] ^ (CORES * j + e)]


def turn_apart(place, signal, blocks):
    rows, width = signal.shape
    cols = width // 2
    shape = (cols // blocks, rows)
    pairs = blocks // CORES
    return pl.pallas_call(
        turn_apart_kernel,
        grid=(1,),
        in_specs=[
            pl.BlockSpec(memory_space=pltpu.SMEM),
            pl.BlockSpec((rows, cols), lambda i: (0, 1)),
        ],
        out_specs=[pl.BlockSpec((CORES, *shape), lambda i: (0, 0, 0))] * pairs,
        out_shape=[jax.ShapeDtypeStruct((CORES, *shape), jnp.float32)] * pairs,
        scratch_shapes=[pltpu.VMEM((blocks, *shape), jnp.float32)],
        compiler_params=pltpu.CompilerParams(vmem_limit_bytes=VMEM_BYTES),
        cost_estimate=pl.CostEstimate(flops=0, bytes_accessed=8 * rows * cols, transcendentals=0),
        name="turn_apart",
    )(place, signal)


def home_kernel(back_ref, sig_ref, gain_ref, *rest):
    rest[-1][...] = turned(back_ref) + gain_ref[...] * sig_ref[...]


def home(back, signal, gain, start, partial_out):
    rows, width = signal.shape
    cols = back.shape[0]
    step = math.gcd(start, cols)
    here = lambda i: (0, start // step + i)
    in_specs = [
        pl.BlockSpec((step, rows), lambda i: (i, 0)),
        pl.BlockSpec((rows, step), here),
        pl.BlockSpec((1, step), here),
    ]
    operands = [back, signal, gain]
    aliases = {}
    if partial_out is not None:
        in_specs.append(pl.BlockSpec(memory_space=pl.ANY))
        operands.append(partial_out)
        aliases = {3: 0}
    return pl.pallas_call(
        home_kernel,
        grid=(cols // step,),
        in_specs=in_specs,
        out_specs=pl.BlockSpec((rows, step), here),
        out_shape=jax.ShapeDtypeStruct((rows, width), jnp.float32),
        input_output_aliases=aliases,
        compiler_params=pltpu.CompilerParams(vmem_limit_bytes=VMEM_BYTES),
        cost_estimate=pl.CostEstimate(flops=0, bytes_accessed=12 * rows * cols, transcendentals=0),
        name="home",
    )(*operands)


def shifted_taps(side, group, own_ref, other_ref, high_ref, low_ref):
    blocks = own_ref.shape[0]

    def line(ref, q):
        return jnp.broadcast_to(ref[q, pl.ds(group, 1), :], (8, HALF))

    lines = []
    for q in range(blocks):
        own, other = line(own_ref, q), line(other_ref, q)
        lines += [jnp.where(side == 0, own, other), jnp.where(side == 0, other, own)]
    blank = jnp.zeros((8, HALF), jnp.float32)
    strip = jnp.concatenate([blank] + lines + [blank], axis=1)
    strip = pltpu.roll(strip, 0, 1, stride=1, stride_axis=0)
    for p in range(HALF // 16):
        pair = jnp.concatenate(
            [pltpu.roll(strip, 16 * p, 1) if p else strip, pltpu.roll(strip, 16 * p + 8, 1)], axis=0
        )
        high, low = split_halves(pair)
        high_ref[16 * p : 16 * p + 16, :] = high
        low_ref[16 * p : 16 * p + 16, :] = low


def causal_sums(signal, high_ref, low_ref, sum_ref):
    rows = signal.shape[1]
    blocks = signal.shape[0] // GROUP
    sig_high, sig_low = split_halves(signal)

    def window(ref, lag_block):
        start = lag_block * rows
        return jnp.concatenate(
            [ref[:, start + HALF * k : start + HALF * k + rows] for k in (1, 0)], axis=0
        )

    for d in range(blocks):
        n = (blocks - d) * GROUP
        taps_high, taps_low = window(high_ref, d), window(low_ref, d)
        both = jnp.concatenate([sig_high[:n], sig_low[:n]], axis=0)
        part = jnp.dot(both, taps_high, preferred_element_type=jnp.float32)
        term = part[:n] + part[n:]
        term = term + jnp.dot(sig_high[:n], taps_low, preferred_element_type=jnp.float32)
        if d == 0:
            sum_ref[...] = term
        else:
            sum_ref[d * GROUP :, :] += term


def conv_kernel(first, place_ref, own_ref, other_ref, sig_ref, *rest):
    out_ref, scratch = rest[0], rest[-3 * PAIR :]
    blocks, _, rows = sig_ref.shape
    for u in range(PAIR):
        group = first + PAIR * pl.program_id(0) + u
        shifted_taps(place_ref[1], group, own_ref, other_ref, scratch[3 * u], scratch[3 * u + 1])
    for u in range(PAIR):
        high_ref, low_ref, sum_ref = scratch[3 * u : 3 * u + 3]
        at = slice(u * GROUP, (u + 1) * GROUP)
        causal_sums(sig_ref[:, at, :].reshape(blocks * GROUP, rows), high_ref, low_ref, sum_ref)
        out_ref[:, at, :] = sum_ref[...].reshape(blocks, GROUP, rows)


def conv_apart_kernel(first, pairs, place_ref, own_ref, other_ref, passed_ref, *rest):
    blocks = CORES * pairs
    sigs, outs, hold_ref = rest[:pairs], rest[pairs : pairs + blocks], rest[pairs + blocks]
    scratch = rest[pairs + blocks + 1 :]
    rows = hold_ref.shape[2]
    me, side = place_ref[0], place_ref[1]
    for j, sig_ref in enumerate(sigs):
        hold_ref[me ^ (CORES * j)] = sig_ref[0]
        hold_ref[me ^ (CORES * j + 1)] = passed_ref[j]
    for u in range(PAIR):
        group = first + PAIR * pl.program_id(0) + u
        shifted_taps(side, group, own_ref, other_ref, scratch[3 * u], scratch[3 * u + 1])
    for u in range(PAIR):
        high_ref, low_ref, sum_ref = scratch[3 * u : 3 * u + 3]
        at = slice(u * GROUP, (u + 1) * GROUP)
        causal_sums(hold_ref[:, at, :].reshape(blocks * GROUP, rows), high_ref, low_ref, sum_ref)
        for j in range(blocks):
            row = pl.multiple_of((me ^ j) * GROUP, GROUP)
            outs[j][at, :] = sum_ref[pl.ds(row, GROUP), :]


def conv_scratch(blocks, rows):
    lanes = blocks * rows + 2 * HALF
    return [
        pltpu.VMEM((HALF, lanes), jnp.bfloat16),
        pltpu.VMEM((HALF, lanes), jnp.bfloat16),
        pltpu.VMEM((blocks * GROUP, rows), jnp.float32),
    ] * PAIR


def conv_cost(blocks, groups, rows):
    return pl.CostEstimate(
        flops=3 * groups * GROUP * rows * rows * blocks * (blocks + 1),
        bytes_accessed=8 * blocks * groups * GROUP * rows,
        transcendentals=0,
    )


def convolve(place, own, other, arrived, first, groups):
    blocks, _, rows = arrived.shape
    spec = pl.BlockSpec((blocks, PAIR * GROUP, rows), lambda g: (0, g, 0))
    taps_spec = pl.BlockSpec(own.shape, lambda g: (0, 0, 0))
    return pl.pallas_call(
        functools.partial(conv_kernel, first),
        grid=(groups // PAIR,),
        in_specs=[pl.BlockSpec(memory_space=pltpu.SMEM), taps_spec, taps_spec, spec],
        out_specs=spec,
        out_shape=jax.ShapeDtypeStruct((blocks, groups * GROUP, rows), jnp.float32),
        scratch_shapes=conv_scratch(blocks, rows),
        compiler_params=pltpu.CompilerParams(vmem_limit_bytes=VMEM_BYTES),
        cost_estimate=conv_cost(blocks, groups, rows),
        name="convolve",
    )(place, own, other, arrived)


def convolve_apart(place, own, other, passed, parts, first):
    pairs, deep, rows = passed.shape
    blocks = CORES * pairs
    groups = deep // GROUP
    taps_spec = pl.BlockSpec(own.shape, lambda g: (0, 0, 0))
    return pl.pallas_call(
        functools.partial(conv_apart_kernel, first, pairs),
        grid=(groups // PAIR,),
        in_specs=[
            pl.BlockSpec(memory_space=pltpu.SMEM),
            taps_spec,
            taps_spec,
            pl.BlockSpec((pairs, PAIR * GROUP, rows), lambda g: (0, g, 0)),
        ]
        + [pl.BlockSpec((1, PAIR * GROUP, rows), lambda g: (0, g, 0))] * pairs,
        out_specs=[pl.BlockSpec((PAIR * GROUP, rows), lambda g: (g, 0))] * blocks,
        out_shape=[jax.ShapeDtypeStruct((deep, rows), jnp.float32)] * blocks,
        scratch_shapes=[pltpu.VMEM((blocks, PAIR * GROUP, rows), jnp.float32)]
        + conv_scratch(blocks, rows),
        compiler_params=pltpu.CompilerParams(vmem_limit_bytes=VMEM_BYTES),
        cost_estimate=conv_cost(blocks, groups, rows),
        name="convolve_apart",
    )(place, own, other, passed, *parts)


def home_apart_kernel(place_ref, *rest):
    back_refs, (sig_ref, gain_ref, _, out_ref, hold_ref) = rest[:-5], rest[-5:]
    me = place_ref[0]
    for j, back_ref in enumerate(back_refs):
        hold_ref[me ^ j] = back_ref[...]
    values = hold_ref[...].reshape(sig_ref.shape[1], sig_ref.shape[0])
    out_ref[...] = values.T + gain_ref[...] * sig_ref[...]


def home_apart(place, backs, signal, gain, partial_out):
    rows, width = signal.shape
    blocks, per_chunk = len(backs), backs[0].shape[0]
    cols = blocks * per_chunk
    here = lambda i: (0, 1)
    return pl.pallas_call(
        home_apart_kernel,
        grid=(1,),
        in_specs=[pl.BlockSpec(memory_space=pltpu.SMEM)]
        + [pl.BlockSpec((per_chunk, rows), lambda i: (0, 0))] * blocks
        + [pl.BlockSpec((rows, cols), here), pl.BlockSpec((1, cols), here)]
        + [pl.BlockSpec(memory_space=pl.ANY)],
        out_specs=pl.BlockSpec((rows, cols), here),
        out_shape=jax.ShapeDtypeStruct((rows, width), jnp.float32),
        input_output_aliases={blocks + 3: 0},
        scratch_shapes=[pltpu.VMEM((blocks, per_chunk, rows), jnp.float32)],
        compiler_params=pltpu.CompilerParams(vmem_limit_bytes=VMEM_BYTES),
        cost_estimate=pl.CostEstimate(flops=0, bytes_accessed=12 * rows * cols, transcendentals=0),
        name="home_apart",
    )(place, *backs, signal, gain, partial_out)


def exchange(values, axis, step):
    size = lax.axis_size(axis)
    return lax.ppermute(values, axis, [(i, i ^ step) for i in range(size)])


def spread(values):
    return lax.all_to_all(values, "seq", split_axis=0, concat_axis=0, tiled=True)


def after(value, *others):
    return lax.optimization_barrier((value, *others))[0]


def scatter(parts, stride):
    return [exchange(part, "seq", stride * j) if j else part for j, part in enumerate(parts)]


def fast_body(signal, filters, skip_gain):
    blocks = lax.axis_size("seq")
    rows, width = signal.shape
    count = width // blocks // GROUP // 2
    side = lax.axis_index("ch")
    place = jnp.stack([lax.axis_index("seq"), side]).astype(jnp.int32)
    gain = skip_gain.reshape(1, width)
    first = spread(turn_taps(signal, filters, blocks, (count, count)))
    raw = turn_apart(place, signal, blocks)
    parts = scatter(raw[:5], CORES)
    first = after(first, *parts[1:4])
    parts += [exchange(after(part, parts[3]), "seq", CORES * (5 + j)) for j, part in enumerate(raw[5:])]
    taps = first[:, count * GROUP :, :]
    own = lax.dynamic_slice_in_dim(taps, side * HALF, HALF, axis=2)
    other = exchange(lax.dynamic_slice_in_dim(taps, (1 - side) * HALF, HALF, axis=2), "ch", 1)
    values = convolve(place, own, other, first, 0, count)
    values = after(values, *parts[1:5])
    back = spread(values).reshape(-1, rows)
    passed = exchange(jnp.stack([part[1] for part in parts]), "seq", 1)
    parts = scatter(convolve_apart(place, own, other, passed, parts, count), 1)
    out = home(back, signal, gain, 0, None)
    return home_apart(place, parts, signal, gain, out)


def angle_table(row_count, col_count, length, sign):
    row_index = jnp.arange(row_count, dtype=jnp.int32)[:, None]
    col_index = jnp.arange(col_count, dtype=jnp.int32)[None, :]
    phase = row_index * col_index % length
    angle = sign * 2.0 * math.pi / length * phase.astype(jnp.float32)
    return (jnp.cos(angle), jnp.sin(angle))


def complex_apply(form, table, real_part, imag_part):
    cosine, sine = table

    def product(matrix, values):
        return jnp.einsum(form, matrix, values, precision=HIGHEST_PRECISION)

    if imag_part is None:
        return (product(cosine, real_part), product(sine, real_part))
    return (
        product(cosine, real_part) - product(sine, imag_part),
        product(cosine, imag_part) + product(sine, real_part),
    )


def rotate(real_part, imag_part, cosine, sine):
    return (real_part * cosine - imag_part * sine, real_part * sine + imag_part * cosine)


def local_convolve(whole_sig, whole_taps, blocks, rows):
    width = whole_sig.shape[1]
    span = 2 * blocks * rows
    sig_blocks = whole_sig.reshape(blocks, rows, width)
    tap_blocks = whole_taps.reshape(blocks, rows, width)
    outer = angle_table(2 * blocks, blocks, 2 * blocks, -1.0)
    sig_real, sig_imag = complex_apply("kn,nbc->kbc", outer, sig_blocks, None)
    filt_real, filt_imag = complex_apply("kn,nbc->kbc", outer, tap_blocks, None)
    phase = (
        jnp.arange(2 * blocks, dtype=jnp.int32)[:, None]
        * jnp.arange(rows, dtype=jnp.int32)[None, :]
        % span
    )
    twist = 2.0 * math.pi / span * phase.astype(jnp.float32)
    twist_cos = jnp.cos(twist)[:, :, None]
    twist_sin = jnp.sin(twist)[:, :, None]
    sig_real, sig_imag = rotate(sig_real, sig_imag, twist_cos, -twist_sin)
    filt_real, filt_imag = rotate(filt_real, filt_imag, twist_cos, -twist_sin)
    inner = angle_table(rows, rows, rows, -1.0)
    sig_real, sig_imag = complex_apply("kn,bnc->bkc", inner, sig_real, sig_imag)
    filt_real, filt_imag = complex_apply("kn,bnc->bkc", inner, filt_real, filt_imag)
    prod_real, prod_imag = rotate(sig_real, sig_imag, filt_real, filt_imag)
    inverse_inner = angle_table(rows, rows, rows, 1.0)
    back_real, back_imag = complex_apply("nk,bkc->bnc", inverse_inner, prod_real, prod_imag)
    back_real, back_imag = rotate(back_real, back_imag, twist_cos, twist_sin)
    outer_back = angle_table(blocks, 2 * blocks, 2 * blocks, 1.0)
    values = jnp.einsum(
        "nk,kbc->nbc", outer_back[0], back_real, precision=HIGHEST_PRECISION
    ) - jnp.einsum("nk,kbc->nbc", outer_back[1], back_imag, precision=HIGHEST_PRECISION)
    return values.reshape(blocks * rows, width) / span


def spectral_body(signal, filters, skip_gain):
    blocks = lax.axis_size("seq")
    rows = signal.shape[0]
    taps = lax.all_to_all(filters, "ch", split_axis=1, concat_axis=0, tiled=True)
    local_groups = taps.shape[1]
    per_channel = jnp.broadcast_to(taps[:, :, None], (rows, local_groups, GROUP)).reshape(
        rows, local_groups * GROUP
    )
    whole_sig, whole_taps = (
        lax.all_to_all(signal, "seq", split_axis=1, concat_axis=0, tiled=True),
        lax.all_to_all(per_channel, "seq", split_axis=1, concat_axis=0, tiled=True),
    )
    values = local_convolve(whole_sig, whole_taps, blocks, rows)
    homed = lax.all_to_all(values, "seq", split_axis=0, concat_axis=1, tiled=True)
    return homed + skip_gain[None, :] * signal


def body(signal, filters, skip_gain):
    blocks = lax.axis_size("seq")
    rows, width = signal.shape
    lag_rows = filters.shape[0]
    fits = (
        blocks >= 2 * CORES
        and blocks & (blocks - 1) == 0
        and lax.axis_size("ch") == 2
        and width % (blocks * 2 * PAIR * GROUP) == 0
        and rows == 2 * HALF
        and lag_rows == HALF
    )
    if fits:
        return fast_body(signal, filters, skip_gain)
    return spectral_body(signal, filters, skip_gain)


def solution(mesh):
    placed = (P("seq", "ch"), P(("seq", "ch"), None), P("ch"))
    return jax.shard_map(
        body, mesh=mesh, in_specs=placed, out_specs=P("seq", "ch"), check_vma=False
    )
```

```python
import functools
import math

import jax
import jax.numpy as jnp
from jax import lax
from jax.experimental import pallas as pl
from jax.experimental.pallas import tpu as pltpu
from jax.sharding import PartitionSpec as P

GROUP = 16
HALF = 128
PAIR = 2
CORES = 2
STEPS = 2
VMEM_BYTES = 60 * 1024 * 1024

HIGHEST_PRECISION = lax.Precision.HIGHEST


def split_halves(values):
    high = values.astype(jnp.bfloat16)
    low = (values - high.astype(jnp.float32)).astype(jnp.bfloat16)
    return high, low


def turned(in_ref):
    return in_ref[...].T


def turn_taps_kernel(counts, sig_ref, taps_ref, out_ref, lines_ref):
    homes, _, rows = out_ref.shape
    per_chunk = sig_ref.shape[1] // homes
    lag_rows, groups = taps_ref.shape
    out_ref[:, :per_chunk, :] = turned(sig_ref).reshape(homes, per_chunk, rows)
    lines_ref[...] = turned(taps_ref)
    sides = rows // lag_rows
    for side in range(sides):
        row = per_chunk
        start = side * (groups // sides)
        for count in counts:
            here = start + pl.program_id(0) * (homes * count)
            lines = lines_ref[pl.ds(pl.multiple_of(here, 8), homes * count), :]
            at = slice(side * lag_rows, (side + 1) * lag_rows)
            for q in range(homes):
                out_ref[q, row : row + count, at] = lines[q * count : (q + 1) * count]
            row += count
            start += homes * pl.num_programs(0) * count


def turn_taps(signal, filters, blocks, counts):
    rows, width = signal.shape
    cols = blocks * counts[0] * GROUP
    deep = counts[0] * GROUP + sum(counts)
    return pl.pallas_call(
        functools.partial(turn_taps_kernel, counts),
        grid=(STEPS,),
        in_specs=[
            pl.BlockSpec((rows, cols // STEPS), lambda i: (0, i)),
            pl.BlockSpec(filters.shape, lambda i: (0, 0)),
        ],
        out_specs=pl.BlockSpec((blocks // STEPS, deep, rows), lambda i: (i, 0, 0)),
        out_shape=jax.ShapeDtypeStruct((blocks, deep, rows), jnp.float32),
        scratch_shapes=[pltpu.VMEM(filters.shape[::-1], jnp.float32)],
        compiler_params=pltpu.CompilerParams(vmem_limit_bytes=VMEM_BYTES),
        cost_estimate=pl.CostEstimate(flops=0, bytes_accessed=8 * rows * cols, transcendentals=0),
        name="turn_taps",
    )(signal, filters)


def turn_apart_kernel(place_ref, sig_ref, *rest):
    outs, hold_ref = rest[:-1], rest[-1]
    hold_ref[...] = turned(sig_ref).reshape(hold_ref.shape)
    for j, out_ref in enumerate(outs):
        for e in range(CORES):
            out_ref[e] = hold_ref[place_ref[0] ^ (CORES * j + e)]


def turn_apart(place, signal, blocks):
    rows, width = signal.shape
    cols = width // 2
    shape = (cols // blocks, rows)
    pairs = blocks // CORES
    return pl.pallas_call(
        turn_apart_kernel,
        grid=(1,),
        in_specs=[
            pl.BlockSpec(memory_space=pltpu.SMEM),
            pl.BlockSpec((rows, cols), lambda i: (0, 1)),
        ],
        out_specs=[pl.BlockSpec((CORES, *shape), lambda i: (0, 0, 0))] * pairs,
        out_shape=[jax.ShapeDtypeStruct((CORES, *shape), jnp.float32)] * pairs,
        scratch_shapes=[pltpu.VMEM((blocks, *shape), jnp.float32)],
        compiler_params=pltpu.CompilerParams(vmem_limit_bytes=VMEM_BYTES),
        cost_estimate=pl.CostEstimate(flops=0, bytes_accessed=8 * rows * cols, transcendentals=0),
        name="turn_apart",
    )(place, signal)


def home_kernel(back_ref, sig_ref, gain_ref, *rest):
    rest[-1][...] = turned(back_ref) + gain_ref[...] * sig_ref[...]


def home(back, signal, gain, start, partial_out):
    rows, width = signal.shape
    cols = back.shape[0]
    step = math.gcd(start, cols)
    here = lambda i: (0, start // step + i)
    in_specs = [
        pl.BlockSpec((step, rows), lambda i: (i, 0)),
        pl.BlockSpec((rows, step), here),
        pl.BlockSpec((1, step), here),
    ]
    operands = [back, signal, gain]
    aliases = {}
    if partial_out is not None:
        in_specs.append(pl.BlockSpec(memory_space=pl.ANY))
        operands.append(partial_out)
        aliases = {3: 0}
    return pl.pallas_call(
        home_kernel,
        grid=(cols // step,),
        in_specs=in_specs,
        out_specs=pl.BlockSpec((rows, step), here),
        out_shape=jax.ShapeDtypeStruct((rows, width), jnp.float32),
        input_output_aliases=aliases,
        compiler_params=pltpu.CompilerParams(vmem_limit_bytes=VMEM_BYTES),
        cost_estimate=pl.CostEstimate(flops=0, bytes_accessed=12 * rows * cols, transcendentals=0),
        name="home",
    )(*operands)


def shifted_taps(side, group, own_ref, other_ref, high_ref, low_ref):
    blocks = own_ref.shape[0]

    def line(ref, q):
        return jnp.broadcast_to(ref[q, pl.ds(group, 1), :], (8, HALF))

    lines = []
    for q in range(blocks):
        own, other = line(own_ref, q), line(other_ref, q)
        lines += [jnp.where(side == 0, own, other), jnp.where(side == 0, other, own)]
    blank = jnp.zeros((8, HALF), jnp.float32)
    strip = jnp.concatenate([blank] + lines + [blank], axis=1)
    strip = pltpu.roll(strip, 0, 1, stride=1, stride_axis=0)
    for p in range(HALF // 16):
        pair = jnp.concatenate(
            [pltpu.roll(strip, 16 * p, 1) if p else strip, pltpu.roll(strip, 16 * p + 8, 1)], axis=0
        )
        high, low = split_halves(pair)
        high_ref[16 * p : 16 * p + 16, :] = high
        low_ref[16 * p : 16 * p + 16, :] = low


def causal_sums(signal, high_ref, low_ref, sum_ref):
    rows = signal.shape[1]
    blocks = signal.shape[0] // GROUP
    sig_high, sig_low = split_halves(signal)

    def window(ref, lag_block):
        start = lag_block * rows
        return jnp.concatenate(
            [ref[:, start + HALF * k : start + HALF * k + rows] for k in (1, 0)], axis=0
        )

    for d in range(blocks):
        n = (blocks - d) * GROUP
        taps_high, taps_low = window(high_ref, d), window(low_ref, d)
        both = jnp.concatenate([sig_high[:n], sig_low[:n]], axis=0)
        part = jnp.dot(both, taps_high, preferred_element_type=jnp.float32)
        term = part[:n] + part[n:]
        term = term + jnp.dot(sig_high[:n], taps_low, preferred_element_type=jnp.float32)
        if d == 0:
            sum_ref[...] = term
        else:
            sum_ref[d * GROUP :, :] += term


def conv_kernel(first, place_ref, own_ref, other_ref, sig_ref, *rest):
    out_ref, scratch = rest[0], rest[-3 * PAIR :]
    blocks, _, rows = sig_ref.shape
    for u in range(PAIR):
        group = first + PAIR * pl.program_id(0) + u
        shifted_taps(place_ref[1], group, own_ref, other_ref, scratch[3 * u], scratch[3 * u + 1])
    for u in range(PAIR):
        high_ref, low_ref, sum_ref = scratch[3 * u : 3 * u + 3]
        at = slice(u * GROUP, (u + 1) * GROUP)
        causal_sums(sig_ref[:, at, :].reshape(blocks * GROUP, rows), high_ref, low_ref, sum_ref)
        out_ref[:, at, :] = sum_ref[...].reshape(blocks, GROUP, rows)


def conv_apart_kernel(first, pairs, place_ref, own_ref, other_ref, passed_ref, *rest):
    blocks = CORES * pairs
    sigs, outs, hold_ref = rest[:pairs], rest[pairs : pairs + blocks], rest[pairs + blocks]
    scratch = rest[pairs + blocks + 1 :]
    rows = hold_ref.shape[2]
    me, side = place_ref[0], place_ref[1]
    for j, sig_ref in enumerate(sigs):
        hold_ref[me ^ (CORES * j)] = sig_ref[0]
        hold_ref[me ^ (CORES * j + 1)] = passed_ref[j]
    for u in range(PAIR):
        group = first + PAIR * pl.program_id(0) + u
        shifted_taps(side, group, own_ref, other_ref, scratch[3 * u], scratch[3 * u + 1])
    for u in range(PAIR):
        high_ref, low_ref, sum_ref = scratch[3 * u : 3 * u + 3]
        at = slice(u * GROUP, (u + 1) * GROUP)
        causal_sums(hold_ref[:, at, :].reshape(blocks * GROUP, rows), high_ref, low_ref, sum_ref)
        for j in range(blocks):
            row = pl.multiple_of((me ^ j) * GROUP, GROUP)
            outs[j][at, :] = sum_ref[pl.ds(row, GROUP), :]


def conv_scratch(blocks, rows):
    lanes = blocks * rows + 2 * HALF
    return [
        pltpu.VMEM((HALF, lanes), jnp.bfloat16),
        pltpu.VMEM((HALF, lanes), jnp.bfloat16),
        pltpu.VMEM((blocks * GROUP, rows), jnp.float32),
    ] * PAIR


def conv_cost(blocks, groups, rows):
    return pl.CostEstimate(
        flops=3 * groups * GROUP * rows * rows * blocks * (blocks + 1),
        bytes_accessed=8 * blocks * groups * GROUP * rows,
        transcendentals=0,
    )


def convolve(place, own, other, arrived, first, groups):
    blocks, _, rows = arrived.shape
    spec = pl.BlockSpec((blocks, PAIR * GROUP, rows), lambda g: (0, g, 0))
    taps_spec = pl.BlockSpec(own.shape, lambda g: (0, 0, 0))
    return pl.pallas_call(
        functools.partial(conv_kernel, first),
        grid=(groups // PAIR,),
        in_specs=[pl.BlockSpec(memory_space=pltpu.SMEM), taps_spec, taps_spec, spec],
        out_specs=spec,
        out_shape=jax.ShapeDtypeStruct((blocks, groups * GROUP, rows), jnp.float32),
        scratch_shapes=conv_scratch(blocks, rows),
        compiler_params=pltpu.CompilerParams(vmem_limit_bytes=VMEM_BYTES),
        cost_estimate=conv_cost(blocks, groups, rows),
        name="convolve",
    )(place, own, other, arrived)


def convolve_apart(place, own, other, passed, parts, first):
    pairs, deep, rows = passed.shape
    blocks = CORES * pairs
    groups = deep // GROUP
    taps_spec = pl.BlockSpec(own.shape, lambda g: (0, 0, 0))
    return pl.pallas_call(
        functools.partial(conv_apart_kernel, first, pairs),
        grid=(groups // PAIR,),
        in_specs=[
            pl.BlockSpec(memory_space=pltpu.SMEM),
            taps_spec,
            taps_spec,
            pl.BlockSpec((pairs, PAIR * GROUP, rows), lambda g: (0, g, 0)),
        ]
        + [pl.BlockSpec((1, PAIR * GROUP, rows), lambda g: (0, g, 0))] * pairs,
        out_specs=[pl.BlockSpec((PAIR * GROUP, rows), lambda g: (g, 0))] * blocks,
        out_shape=[jax.ShapeDtypeStruct((deep, rows), jnp.float32)] * blocks,
        scratch_shapes=[pltpu.VMEM((blocks, PAIR * GROUP, rows), jnp.float32)]
        + conv_scratch(blocks, rows),
        compiler_params=pltpu.CompilerParams(vmem_limit_bytes=VMEM_BYTES),
        cost_estimate=conv_cost(blocks, groups, rows),
        name="convolve_apart",
    )(place, own, other, passed, *parts)


def home_apart_kernel(place_ref, *rest):
    back_refs, (sig_ref, gain_ref, _, out_ref, hold_ref) = rest[:-5], rest[-5:]
    me = place_ref[0]
    step = pl.program_id(0)

    @pl.when(step == 0)
    def _():
        for j, back_ref in enumerate(back_refs):
            hold_ref[me ^ j] = back_ref[...]

    homes = hold_ref.shape[0] // STEPS
    values = hold_ref[pl.ds(step * homes, homes)].reshape(sig_ref.shape[1], sig_ref.shape[0])
    out_ref[...] = values.T + gain_ref[...] * sig_ref[...]


def home_apart(place, backs, signal, gain, partial_out):
    rows, width = signal.shape
    blocks, per_chunk = len(backs), backs[0].shape[0]
    cols = blocks * per_chunk
    here = lambda i: (0, STEPS + i)
    return pl.pallas_call(
        home_apart_kernel,
        grid=(STEPS,),
        in_specs=[pl.BlockSpec(memory_space=pltpu.SMEM)]
        + [pl.BlockSpec((per_chunk, rows), lambda i: (0, 0))] * blocks
        + [pl.BlockSpec((rows, cols // STEPS), here), pl.BlockSpec((1, cols // STEPS), here)]
        + [pl.BlockSpec(memory_space=pl.ANY)],
        out_specs=pl.BlockSpec((rows, cols // STEPS), here),
        out_shape=jax.ShapeDtypeStruct((rows, width), jnp.float32),
        input_output_aliases={blocks + 3: 0},
        scratch_shapes=[pltpu.VMEM((blocks, per_chunk, rows), jnp.float32)],
        compiler_params=pltpu.CompilerParams(vmem_limit_bytes=VMEM_BYTES),
        cost_estimate=pl.CostEstimate(flops=0, bytes_accessed=12 * rows * cols, transcendentals=0),
        name="home_apart",
    )(place, *backs, signal, gain, partial_out)


def exchange(values, axis, step):
    size = lax.axis_size(axis)
    return lax.ppermute(values, axis, [(i, i ^ step) for i in range(size)])


def spread(values):
    return lax.all_to_all(values, "seq", split_axis=0, concat_axis=0, tiled=True)


def after(value, *others):
    return lax.optimization_barrier((value, *others))[0]


def scatter(parts, stride):
    return [exchange(part, "seq", stride * j) if j else part for j, part in enumerate(parts)]


def fast_body(signal, filters, skip_gain):
    blocks = lax.axis_size("seq")
    rows, width = signal.shape
    count = width // blocks // GROUP // 2
    side = lax.axis_index("ch")
    place = jnp.stack([lax.axis_index("seq"), side]).astype(jnp.int32)
    gain = skip_gain.reshape(1, width)
    first = spread(turn_taps(signal, filters, blocks, (count, count)))
    raw = turn_apart(place, signal, blocks)
    parts = scatter(raw[:5], CORES)
    first = after(first, *parts[1:4])
    parts += [exchange(after(part, parts[3]), "seq", CORES * (5 + j)) for j, part in enumerate(raw[5:])]
    taps = first[:, count * GROUP :, :]
    own = lax.dynamic_slice_in_dim(taps, side * HALF, HALF, axis=2)
    other = exchange(lax.dynamic_slice_in_dim(taps, (1 - side) * HALF, HALF, axis=2), "ch", 1)
    values = convolve(place, own, other, first, 0, count)
    values = after(values, *parts[1:5])
    back = spread(values).reshape(-1, rows)
    passed = exchange(jnp.stack([part[1] for part in parts]), "seq", 1)
    parts = scatter(convolve_apart(place, own, other, passed, parts, count), 1)
    out = home(back, signal, gain, 0, None)
    return home_apart(place, parts, signal, gain, out)


def angle_table(row_count, col_count, length, sign):
    row_index = jnp.arange(row_count, dtype=jnp.int32)[:, None]
    col_index = jnp.arange(col_count, dtype=jnp.int32)[None, :]
    phase = row_index * col_index % length
    angle = sign * 2.0 * math.pi / length * phase.astype(jnp.float32)
    return (jnp.cos(angle), jnp.sin(angle))


def complex_apply(form, table, real_part, imag_part):
    cosine, sine = table

    def product(matrix, values):
        return jnp.einsum(form, matrix, values, precision=HIGHEST_PRECISION)

    if imag_part is None:
        return (product(cosine, real_part), product(sine, real_part))
    return (
        product(cosine, real_part) - product(sine, imag_part),
        product(cosine, imag_part) + product(sine, real_part),
    )


def rotate(real_part, imag_part, cosine, sine):
    return (real_part * cosine - imag_part * sine, real_part * sine + imag_part * cosine)


def local_convolve(whole_sig, whole_taps, blocks, rows):
    width = whole_sig.shape[1]
    span = 2 * blocks * rows
    sig_blocks = whole_sig.reshape(blocks, rows, width)
    tap_blocks = whole_taps.reshape(blocks, rows, width)
    outer = angle_table(2 * blocks, blocks, 2 * blocks, -1.0)
    sig_real, sig_imag = complex_apply("kn,nbc->kbc", outer, sig_blocks, None)
    filt_real, filt_imag = complex_apply("kn,nbc->kbc", outer, tap_blocks, None)
    phase = (
        jnp.arange(2 * blocks, dtype=jnp.int32)[:, None]
        * jnp.arange(rows, dtype=jnp.int32)[None, :]
        % span
    )
    twist = 2.0 * math.pi / span * phase.astype(jnp.float32)
    twist_cos = jnp.cos(twist)[:, :, None]
    twist_sin = jnp.sin(twist)[:, :, None]
    sig_real, sig_imag = rotate(sig_real, sig_imag, twist_cos, -twist_sin)
    filt_real, filt_imag = rotate(filt_real, filt_imag, twist_cos, -twist_sin)
    inner = angle_table(rows, rows, rows, -1.0)
    sig_real, sig_imag = complex_apply("kn,bnc->bkc", inner, sig_real, sig_imag)
    filt_real, filt_imag = complex_apply("kn,bnc->bkc", inner, filt_real, filt_imag)
    prod_real, prod_imag = rotate(sig_real, sig_imag, filt_real, filt_imag)
    inverse_inner = angle_table(rows, rows, rows, 1.0)
    back_real, back_imag = complex_apply("nk,bkc->bnc", inverse_inner, prod_real, prod_imag)
    back_real, back_imag = rotate(back_real, back_imag, twist_cos, twist_sin)
    outer_back = angle_table(blocks, 2 * blocks, 2 * blocks, 1.0)
    values = jnp.einsum(
        "nk,kbc->nbc", outer_back[0], back_real, precision=HIGHEST_PRECISION
    ) - jnp.einsum("nk,kbc->nbc", outer_back[1], back_imag, precision=HIGHEST_PRECISION)
    return values.reshape(blocks * rows, width) / span


def spectral_body(signal, filters, skip_gain):
    blocks = lax.axis_size("seq")
    rows = signal.shape[0]
    taps = lax.all_to_all(filters, "ch", split_axis=1, concat_axis=0, tiled=True)
    local_groups = taps.shape[1]
    per_channel = jnp.broadcast_to(taps[:, :, None], (rows, local_groups, GROUP)).reshape(
        rows, local_groups * GROUP
    )
    whole_sig, whole_taps = (
        lax.all_to_all(signal, "seq", split_axis=1, concat_axis=0, tiled=True),
        lax.all_to_all(per_channel, "seq", split_axis=1, concat_axis=0, tiled=True),
    )
    values = local_convolve(whole_sig, whole_taps, blocks, rows)
    homed = lax.all_to_all(values, "seq", split_axis=0, concat_axis=1, tiled=True)
    return homed + skip_gain[None, :] * signal


def body(signal, filters, skip_gain):
    blocks = lax.axis_size("seq")
    rows, width = signal.shape
    lag_rows = filters.shape[0]
    fits = (
        blocks >= 2 * CORES
        and blocks & (blocks - 1) == 0
        and lax.axis_size("ch") == 2
        and width % (blocks * 2 * PAIR * GROUP) == 0
        and rows == 2 * HALF
        and lag_rows == HALF
        and width % (2 * STEPS * HALF) == 0
        and blocks % STEPS == 0
    )
    if fits:
        return fast_body(signal, filters, skip_gain)
    return spectral_body(signal, filters, skip_gain)


def solution(mesh):
    placed = (P("seq", "ch"), P(("seq", "ch"), None), P("ch"))
    return jax.shard_map(
        body, mesh=mesh, in_specs=placed, out_specs=P("seq", "ch"), check_vma=False
    )
```
